256 devices in a mesh: slab: 32 (over x, z), col: 8 (over y, core).
Axes of the slice: x: 4, y: 4, z: 8, core: 2. Of those that a mesh axis runs over, the one named last changes fastest.
Arguments:
- positions: float32 [32, 8, 3, 128], P('slab', 'col'), may hold values from 0 to 1
- atom_types: int32 [32, 8, 128], P('slab', 'col'), may hold values from 0 to 3
- atom_counts: int32 [32, 8], P('slab', 'col'), may hold values from 32 to 128, as said below
- neighbours: int32 [32, 8, 128, 64], P('slab', 'col'), may hold values from -1 to 1151, as said below
- centroid_owner_atoms: int32 [32, 8, 32], P('slab', 'col'), may hold values from -1 to 127, as said below
- centroid_cell_offsets: float32 [32, 8, 3, 32], P('slab', 'col'), may hold values from -0.5 to 0.5
- emb_first: float32 [25, 5], replicated, may hold values from -4 to 4
- emb_second: float32 [50, 25], replicated, may hold values from -1.25 to 1.25
- emb_second_bias: float32 [50], replicated, may hold values from -3 to 3
- emb_third: float32 [100, 50], replicated, may hold values from -0.875 to 0.875
- emb_third_bias: float32 [100], replicated, may hold values from -3 to 3
- fit_first: float32 [240, 1600], replicated, may hold values from -0.15625 to 0.15625
- fit_type: float32 [240, 4], replicated, may hold values from -3 to 3
- fit_second: float32 [240, 240], replicated, may hold values from -0.375 to 0.375
- fit_second_bias: float32 [240], replicated, may hold values from -3 to 3
- fit_out: float32 [240], replicated, may hold values from -0.375 to 0.375
Outputs:
- energy: float32 [], replicated
- forces: float32 [32, 8, 3, 128], P('slab', 'col')
- centroid_force: float32 [32, 8, 3, 32], P('slab', 'col')
The draws below stay inside these ranges and needn't reach their ends.
Inputs may be any that keep to these rules, and one draw needn't show every extreme that they name: `atom_counts`: each count is 128 divided by 1, 2, 3 or 4 and rounded down; some domain holds 128 atoms. `neighbours`: entry k >= 0 names atom k % 128 of the domain at offset (k // 128) // 3 - 1 along slab and (k // 128) % 3 - 1 along col, always a live atom there; -1 pads the tail of every row and fills the rows of slots that are not live. `centroid_owner_atoms`: slot c is live when 4 c is below the domain's count and then names a live atom among 4 c to 4 c + 3; otherwise -1.
All inputs are finite; a program needn't handle non-finite values.
Results may differ from the reference program's by a relative error of at most 0.0003.
Values sent between devices are 32-bit elements; how exact they have to be, the bound alone decides.
No kernel may reach another device: no remote copies, remote signals or barrier semaphores. Data moves between devices by JAX's collectives and lax.ppermute only.
A program may use at most 128 MiB of HBM per device.

```python
import math
import jax
import jax.numpy as jnp
from jax import lax

TYPES = 4
A_DEV = 128
CEN_DEV = 32
NB = 64
EMB1 = 25
EMB2 = 50
EMB3 = 100
AXIS_N = 16
FIT = 240
MZ_DEV = 8
MY_DEV = 32
MESH_X = 256
DOM_Z = 32
DOM_Y = 8
MESH_Z = 256
MESH_Y = 256


def domain_counts(key):
    key = jax.random.fold_in(key, 101)
    first_key, second_key = jax.random.split(key)
    divisor = jax.random.randint(first_key, (DOM_Z, DOM_Y), 1, 5)
    chosen = jax.random.randint(second_key, (), 0, DOM_Z * DOM_Y)
    domain_ids = jnp.arange(DOM_Z * DOM_Y, dtype=jnp.int32).reshape(DOM_Z, DOM_Y)
    divisor = jnp.where(domain_ids == chosen, 1, divisor)
    return (A_DEV // divisor).astype(jnp.int32)


def draw_atom_counts(key, part):
    return domain_counts(key)


def draw_neighbours(key, part):
    counts = domain_counts(key)
    key = jax.random.fold_in(key, 2)
    block_key, atom_key, fill_key = jax.random.split(key, 3)
    mesh_dimensions = (DOM_Z, DOM_Y, A_DEV, NB)
    block_id = jax.random.randint(block_key, mesh_dimensions, 0, 9)
    raw_atom = jax.random.randint(atom_key, mesh_dimensions, 0, 1 << 20)
    row_z = jnp.arange(DOM_Z, dtype=jnp.int32)[:, None, None, None]
    row_y = jnp.arange(DOM_Y, dtype=jnp.int32)[None, :, None, None]
    home_z = (row_z + block_id // 3 - 1) % DOM_Z
    home_y = (row_y + block_id % 3 - 1) % DOM_Y
    atom_id = raw_atom % counts[home_z, home_y]
    filled = jax.random.randint(fill_key, (DOM_Z, DOM_Y, A_DEV, 1), NB // 2, NB + 1)
    slot_ids = jnp.arange(NB, dtype=jnp.int32)[None, None, None, :]
    owner_ids = jnp.arange(A_DEV, dtype=jnp.int32)[None, None, :, None]
    live = (slot_ids < filled) & (owner_ids < counts[:, :, None, None])
    table = jnp.where(live, block_id * A_DEV + atom_id, -1)
    corner_full = counts[(row_z + 1) % DOM_Z, (row_y + 1) % DOM_Y] == A_DEV
    forced = corner_full & (owner_ids == 0) & (slot_ids == 0)
    return jnp.where(forced, 9 * A_DEV - 1, table).astype(jnp.int32)


def draw_centroid_owner_atoms(key, part):
    counts = domain_counts(key)
    key = jax.random.fold_in(key, 3)
    first_atom = 4 * jnp.arange(CEN_DEV, dtype=jnp.int32)[None, None, :]
    room = jnp.clip(counts[:, :, None] - first_atom, 1, 4)
    offset = jax.random.randint(key, (DOM_Z, DOM_Y, CEN_DEV), 0, 4) % room
    last_full = (counts[:, :, None] == A_DEV) & (first_atom == A_DEV - 4)
    offset = jnp.where(last_full, 3, offset)
    return jnp.where(first_atom < counts[:, :, None], first_atom + offset, -1).astype(jnp.int32)


def place_ends(result, rng, low, top_value):
    index_at = [jax.random.randint(jax.random.fold_in(rng, axis), (), 0, length) for axis, length in enumerate(result.shape)]
    longest = result.shape.index(max(result.shape))
    next_to = index_at[:longest] + [(index_at[longest] + 1) % result.shape[longest]] + index_at[longest + 1:]
    return result.at[tuple(index_at)].set(low).at[tuple(next_to)].set(top_value)


def steps_of(stream_key, dims, shards, smallest, high):
    def one(axis_at, blocks):
        draws = jax.random.uniform(jax.random.fold_in(jax.random.fold_in(stream_key, 6), axis_at), (blocks,), jnp.float32, smallest / len(shards), high / len(shards))
        return jnp.repeat(jnp.exp(draws), dims[axis_at] // blocks).reshape((-1,) + (1,) * (len(dims) - axis_at - 1))

    level = one(*shards[0])
    for cut in shards[1:]:
        level = level * one(*cut)
    return level


def normal_values(stream_key, dims, width, reach, cuts=(), held_as=jnp.bfloat16):
    result = jax.random.normal(stream_key, dims, jnp.float32) * width
    if len(cuts) > 0:
        result = steps_of(stream_key, dims, cuts, -0.22, 0.18) * result
    return jnp.clip(result, min=-reach, max=reach).astype(held_as)


def setup_inputs(seed: int = 0) -> dict:
    key_of = jax.random.split(jax.random.key(seed), 17)
    positions = jnp.clip(1.0 * jax.random.uniform(key_of[0], (DOM_Z, DOM_Y, 3, A_DEV), jnp.float32) ** steps_of(key_of[0], (DOM_Z, DOM_Y, 3, A_DEV), ((0, 32), (1, 8)), -0.2, 0.2), 0.0, 1.0)
    atom_types = place_ends(jax.random.randint(key_of[1], (DOM_Z, DOM_Y, A_DEV), 0, TYPES), jax.random.fold_in(key_of[1], 1), 0, TYPES - 1).astype(jnp.int32)
    atom_counts = draw_atom_counts(jax.random.fold_in(key_of[16], 71), 0)
    neighbours = draw_neighbours(jax.random.fold_in(key_of[16], 71), 0)
    centroid_owner_atoms = draw_centroid_owner_atoms(jax.random.fold_in(key_of[16], 71), 0)
    centroid_cell_offsets = normal_values(key_of[5], (DOM_Z, DOM_Y, 3, CEN_DEV), 0.2, 0.5, ((0, 32), (1, 8)), jnp.float32)
    emb_first = normal_values(key_of[6], (EMB1, 1 + TYPES), 1.0, 4.0, (), jnp.float32)
    emb_second = normal_values(key_of[7], (EMB2, EMB1), EMB1 ** -0.5, 1.25, (), jnp.float32)
    emb_second_bias = normal_values(key_of[8], (EMB2,), 1.0, 3.0, (), jnp.float32)
    emb_third = normal_values(key_of[9], (EMB3, EMB2), EMB2 ** -0.5, 0.875, (), jnp.float32)
    emb_third_bias = normal_values(key_of[10], (EMB3,), 1.0, 3.0, (), jnp.float32)
    fit_first = normal_values(key_of[11], (FIT, EMB3 * AXIS_N), (EMB3 * AXIS_N) ** -0.5, 0.15625, (), jnp.float32)
    fit_type = normal_values(key_of[12], (FIT, TYPES), 1.0, 3.0, (), jnp.float32)
    fit_second = normal_values(key_of[13], (FIT, FIT), FIT ** -0.5, 0.375, (), jnp.float32)
    fit_second_bias = normal_values(key_of[14], (FIT,), 1.0, 3.0, (), jnp.float32)
    fit_out = normal_values(key_of[15], (FIT,), FIT ** -0.5, 0.375, (), jnp.float32)
    return {"positions": positions, "atom_types": atom_types, "atom_counts": atom_counts, "neighbours": neighbours, "centroid_owner_atoms": centroid_owner_atoms, "centroid_cell_offsets": centroid_cell_offsets, "emb_first": emb_first, "emb_second": emb_second, "emb_second_bias": emb_second_bias, "emb_third": emb_third, "emb_third_bias": emb_third_bias, "fit_first": fit_first, "fit_type": fit_type, "fit_second": fit_second, "fit_second_bias": fit_second_bias, "fit_out": fit_out}


charge_table = (6.0, 1.0, 1.0, -1.0)
wannier_charge = -8.0
smooth_range = 24.0
coupling = 0.05
smear = 0.6
highest = lax.Precision.HIGHEST

def spline_weights(fraction):
    weights = [fraction, 1.0 - fraction]
    for order_n in range(3, 6):
        earlier = weights
        weights = []
        for term_k in range(order_n):
            total = jnp.zeros_like(fraction)
            if term_k <= order_n - 2:
                total = total + (fraction + term_k) * earlier[term_k]
            if term_k >= 1:
                total = total + (order_n - term_k - fraction) * earlier[term_k - 1]
            weights.append(total / (order_n - 1))
    return weights

def product(left, right):
    return jnp.dot(left, right, precision=highest, preferred_element_type=jnp.float32)

def contract(form, left, right):
    return jnp.einsum(form, left, right, precision=highest)

def embedding(smooth, near_kinds, weights):
    emb_first, emb_second, emb_second_bias, emb_third, emb_third_bias = weights[:5]
    layer_one = jnp.tanh(emb_first[:, :1] * smooth[None, :] + product(emb_first[:, 1:], near_kinds))
    layer_two = jnp.tanh(product(emb_second, layer_one) + emb_second_bias[:, None]) + jnp.concatenate([layer_one, layer_one], 0)
    return jnp.tanh(product(emb_third, layer_two) + emb_third_bias[:, None]) + jnp.concatenate([layer_two, layer_two], 0)

def domain_energy(centre, nearby, near_live, near_kinds, own_kinds, own_live, weights):
    fit_first, fit_type, fit_second, fit_second_bias, fit_out = weights[5:]
    count_of_atoms = centre.shape[1]
    slot_count = nearby.shape[2]
    scaled = (nearby - centre[:, :, None]) / smooth_range
    radius = jnp.sqrt(1.0 + lax.optimization_barrier(jnp.sum(scaled * scaled, 0)))
    smooth = near_live / radius
    envelope = jnp.concatenate([smooth[None], smooth[None] * scaled / radius[None]], 0)
    feature = embedding(smooth.reshape(-1), near_kinds, weights).reshape(-1, count_of_atoms, slot_count)
    moments = contract('cap,map->acm', envelope, feature) / slot_count
    descriptor = contract('acm,acn->amn', moments, moments[:, :, :AXIS_N]).reshape(count_of_atoms, -1)
    hidden = jnp.tanh(contract('fd,ad->fa', fit_first, descriptor) + product(fit_type, own_kinds))
    hidden = hidden + jnp.tanh(product(fit_second, hidden) + fit_second_bias[:, None])
    return jnp.sum(product(fit_out[None, :], hidden)[0] * own_live)

def wave_numbers(index_set, size):
    signed = jnp.where(index_set < size // 2, index_set, index_set - size)
    return signed.astype(jnp.float32) * (2.0 * math.pi / size)

def green_values(wave_z, wave_y, wave_x):
    square = wave_z * wave_z + wave_y * wave_y + wave_x * wave_x
    nonzero = square > 0.0
    safe = jnp.where(nonzero, square, 1.0)
    return jnp.where(nonzero, 4.0 * math.pi * jnp.exp(-0.5 * smear * smear * square) / safe, 0.0)

def mesh_targets(coord, anchor, size):
    floor_c = jnp.floor(coord)
    weights = spline_weights(coord - floor_c)
    start = floor_c.astype(jnp.int32) + anchor
    return [((start + 2 - term_k) % size, weights[term_k]) for term_k in range(5)]

def short_range(cell_pos, atom_types, atom_counts, neighbours, weights):
    slot_ids = jnp.arange(A_DEV, dtype=jnp.int32)
    kind_ids = jnp.arange(TYPES, dtype=jnp.int32)

    def one_domain(domain):
        row_z = domain // DOM_Y
        row_y = domain % DOM_Y
        table = neighbours[row_z, row_y]
        near_live = table >= 0
        entry = jnp.where(near_live, table, 0)
        block_id = entry // A_DEV
        atom_id = entry % A_DEV
        step_z = block_id // 3 - 1
        step_y = block_id % 3 - 1
        home_z = (row_z + step_z) % DOM_Z
        home_y = (row_y + step_y) % DOM_Y
        offset = jnp.stack([jnp.zeros_like(step_y), step_y * MY_DEV, step_z * MZ_DEV]).astype(jnp.float32)
        nearby = jnp.moveaxis(cell_pos[home_z, home_y, :, atom_id], -1, 0) + offset
        near_kinds = (atom_types[home_z, home_y, atom_id].reshape(1, -1) == kind_ids[:, None]).astype(jnp.float32)
        own_kinds = (atom_types[row_z, row_y][None, :] == kind_ids[:, None]).astype(jnp.float32)
        own_live = (slot_ids < atom_counts[row_z, row_y]).astype(jnp.float32)
        return domain_energy(cell_pos[row_z, row_y], nearby, near_live.astype(jnp.float32), near_kinds, own_kinds, own_live, weights)
    return jnp.sum(lax.map(jax.checkpoint(one_domain), jnp.arange(DOM_Z * DOM_Y, dtype=jnp.int32)))

def long_range(cell_pos, wannier_centres, charges):
    atom_positions = jnp.concatenate([cell_pos, wannier_centres], 3)
    anchor_z = (jnp.arange(DOM_Z, dtype=jnp.int32) * MZ_DEV)[:, None, None]
    anchor_y = (jnp.arange(DOM_Y, dtype=jnp.int32) * MY_DEV)[None, :, None]
    along_x = mesh_targets(atom_positions[:, :, 0], 0, MESH_X)
    along_y = mesh_targets(atom_positions[:, :, 1], anchor_y, MESH_Y)
    along_z = mesh_targets(atom_positions[:, :, 2], anchor_z, MESH_Z)
    density = jnp.zeros((MESH_Z, MESH_Y, MESH_X), jnp.float32)
    for cell_z, weight_z in along_z:
        for cell_y, weight_y in along_y:
            amplitude = charges * weight_z * weight_y
            for cell_x, weight_x in along_x:
                density = density.at[cell_z, cell_y, cell_x].add(amplitude * weight_x)
    green = green_values(wave_numbers(jnp.arange(MESH_Z, dtype=jnp.int32), MESH_Z)[:, None, None], wave_numbers(jnp.arange(MESH_Y, dtype=jnp.int32), MESH_Y)[None, :, None], wave_numbers(jnp.arange(MESH_X, dtype=jnp.int32), MESH_X)[None, None, :])
    potential = jnp.real(jnp.fft.ifftn(green * jnp.fft.fftn(density)))
    return 0.5 * coupling * jnp.sum(density * potential)

def reference(positions, atom_types, atom_counts, neighbours, centroid_owner_atoms, centroid_cell_offsets, emb_first, emb_second, emb_second_bias, emb_third, emb_third_bias, fit_first, fit_type, fit_second, fit_second_bias, fit_out):
    weights = (emb_first, emb_second, emb_second_bias, emb_third, emb_third_bias, fit_first, fit_type, fit_second, fit_second_bias, fit_out)
    extent = jnp.array([MESH_X, MY_DEV, MZ_DEV], jnp.float32)
    cell_pos = positions * extent[None, None, :, None]
    slot_ids = jnp.arange(A_DEV, dtype=jnp.int32)
    live = (slot_ids[None, None, :] < atom_counts[:, :, None]).astype(jnp.float32)
    kinds = (atom_types[..., None] == jnp.arange(TYPES, dtype=jnp.int32)).astype(jnp.float32)
    atom_charge = lax.optimization_barrier(jnp.sum(kinds * jnp.array(charge_table, jnp.float32), -1)) * live
    centroid_live = (centroid_owner_atoms >= 0).astype(jnp.float32)
    carrying_atom = jnp.broadcast_to(jnp.maximum(centroid_owner_atoms, 0)[:, :, None, :], centroid_cell_offsets.shape)
    charges = jnp.concatenate([atom_charge, centroid_live * wannier_charge], 2)

    def total_energy(atom_positions, centroid_offset):
        wannier_centres = jnp.take_along_axis(atom_positions, carrying_atom, axis=3) + centroid_offset
        return short_range(atom_positions, atom_types, atom_counts, neighbours, weights) + long_range(atom_positions, wannier_centres, charges)
    total, (cell_grad, shift_grad) = jax.value_and_grad(total_energy, argnums=(0, 1))(cell_pos, centroid_cell_offsets)
    return (total / (DOM_Z * DOM_Y * A_DEV), -cell_grad, -shift_grad)
```

```python
import functools
import math

import jax
import jax.numpy as jnp
import ml_dtypes
import numpy as np
from jax import lax
from jax.experimental import pallas as pl
from jax.experimental.pallas import tpu as pltpu
from jax.sharding import PartitionSpec as P

CHARGES = (6.0, 1.0, 1.0, -1.0)
WANNIER = -8.0
RANGE = 24.0
COUPLING = 0.05
SMEAR = 0.6
ATOMS = 128
CENTRES = 32
SLOTS = 64
MESH = 256
SLABS, COLS = 32, 8
CELL_Z, CELL_Y = 8, 32
REACH = 3
PATCH_Z, PATCH_Y = 14, 40
PATCH = PATCH_Z * PATCH_Y
CHUNK = 640
GROUP = 8
F32 = jnp.float32
BF16 = jnp.bfloat16
BOTH = ("slab", "col")


def halves(array):
    high = array.astype(ml_dtypes.bfloat16)
    low = (array - high.astype(np.float64)).astype(ml_dtypes.bfloat16)
    return high, low


@functools.lru_cache(maxsize=None)
def tables():
    k = np.arange(MESH)[:, None]
    n = np.arange(MESH)[None, :]
    phase = 2.0 * np.pi * ((k * n) % MESH) / MESH
    basis = np.where(k <= MESH // 2, np.cos(phase), np.sin(phase)) * math.sqrt(2.0 / MESH)
    basis[0] = 1.0 / math.sqrt(MESH)
    basis[MESH // 2] = np.where(np.arange(MESH) % 2 == 0, 1.0, -1.0) / math.sqrt(MESH)
    cells_z = (np.arange(PATCH_Z)[:, None] - REACH + CELL_Z * np.arange(SLABS)[None, :]) % MESH
    along_z = basis[:, cells_z.reshape(-1)]
    cells_y = (np.arange(PATCH_Y)[None, :] - REACH + CELL_Y * np.arange(COLS)[:, None]) % MESH
    along_y = basis[:, cells_y.reshape(-1)].T
    out = []
    for matrix in (basis, along_z, along_z.T, along_y, along_y.T):
        out.extend(halves(matrix))
    return out


def split(value):
    high = value.astype(BF16)
    return high, (value - high.astype(F32)).astype(BF16)


def dot(left, right, dims=((1,), (0,))):
    return lax.dot_general(left, right, (dims, ((), ())), preferred_element_type=F32)


def dot3(left, right, dims=((1,), (0,))):
    return dot(left[0], right[0], dims) + (dot(left[0], right[1], dims) + dot(left[1], right[0], dims))


def lanes(table, index):
    return jnp.take_along_axis(table, index, axis=1)


def spline(z, slope):
    a = jnp.abs(z)
    a2 = z * z
    rest = 2.5 - a
    rest2 = rest * rest
    inner = 115.0 / 192.0 + a2 * (-0.625 + 0.25 * a2)
    middle = (55.0 + a * (20.0 + a * (-120.0 + a * (80.0 - 16.0 * a)))) * (1.0 / 96.0)
    outer = rest2 * rest2 * (1.0 / 24.0)
    near, mid, far = a < 0.5, a < 1.5, a < 2.5
    value = jnp.where(near, inner, jnp.where(mid, middle, jnp.where(far, outer, 0.0)))
    if not slope:
        return value, None
    d_inner = a * (a2 - 1.25)
    d_middle = (20.0 + a * (-240.0 + a * (240.0 - 64.0 * a))) * (1.0 / 96.0)
    d_outer = rest2 * rest * (-1.0 / 6.0)
    d = jnp.where(near, d_inner, jnp.where(mid, d_middle, jnp.where(far, d_outer, 0.0)))
    return value, jnp.where(z < 0.0, -d, d)


def points(pos_ref, type_ref, count_ref, owner_ref, shift_ref, place_ref):
    lane = lax.broadcasted_iota(jnp.int32, (8, 128), 1)
    place_ref[...] = jnp.zeros((8, 256), F32)
    place_ref[0:3, 0:128] = pos_ref[...]
    place_ref[0:3, 128:160] = shift_ref[...]
    place_ref[3:4, 128:160] = owner_ref[...].astype(F32)
    row = lax.broadcasted_iota(jnp.int32, (8, 128), 0)
    extent = jnp.where(row == 0, float(MESH), jnp.where(row == 1, float(CELL_Y), float(CELL_Z)))
    atoms = place_ref[:, 0:128] * extent
    owner = jnp.where(lane < CENTRES, place_ref[3:4, 128:256].astype(jnp.int32), -1)
    carrying = jnp.broadcast_to(jnp.maximum(owner, 0), (8, 128))
    centres = lanes(atoms, carrying) + place_ref[:, 128:256]
    kind = type_ref[...]
    charge = jnp.where(
        kind == 0, CHARGES[0], jnp.where(kind == 1, CHARGES[1], jnp.where(kind == 2, CHARGES[2], CHARGES[3]))
    )
    charge = jnp.where(lane[0:1] < count_ref[0, 0], charge, 0.0)
    centre_charge = jnp.where(owner[0:1] >= 0, WANNIER, 0.0)
    place_ref[:, 0:128] = atoms
    place_ref[:, 128:256] = centres
    return jnp.concatenate([charge, centre_charge], axis=1), owner[0:1]


def offsets(coordinate, cells, low):
    cell = lax.broadcasted_iota(jnp.int32, (cells, 256), 0) + low
    return coordinate - cell.astype(F32) - 0.5


def wrapped(z):
    return z - float(MESH) * jnp.round(z * (1.0 / MESH))


def spread_kernel(
    pos_ref, type_ref, count_ref, owner_ref, shift_ref, basis_h, basis_l, out_ref, place_ref, amp_h, amp_l, all_ref
):
    charge, _ = points(pos_ref, type_ref, count_ref, owner_ref, shift_ref, place_ref)
    along_x, _ = spline(wrapped(offsets(place_ref[0:1, :], MESH, 0)), False)
    along_y, _ = spline(offsets(place_ref[1:2, :], PATCH_Y, -REACH), False)
    along_z, _ = spline(offsets(place_ref[2:3, :], 16, -REACH), False)
    along_z = along_z * charge
    for cell in range(PATCH_Z):
        block = along_z[cell : cell + 1, :] * along_y
        high = block.astype(BF16).astype(F32)
        amp_h[cell * PATCH_Y : (cell + 1) * PATCH_Y, :] = high
        amp_l[cell * PATCH_Y : (cell + 1) * PATCH_Y, :] = block - high
    spectral = split(dot3((basis_h[...], basis_l[...]), split(along_x)))
    all_ref[...] = jnp.zeros((MESH, CHUNK), F32)
    all_ref[:, 0:PATCH] = dot3(
        spectral, (amp_h[...].astype(BF16), amp_l[...].astype(BF16)), ((1,), (1,))
    )
    out_ref[:, 0, :] = all_ref[...]


def solve_kernel(
    plane_ref, short_ref, index_ref, z_h, z_l, zt_h, zt_l, y_h, y_l, yt_h, yt_l, out_ref, all_ref, grid_ref
):
    for tile in range(CHUNK // 128):
        all_ref[tile] = plane_ref[:, 0, tile * 128 : (tile + 1) * 128]
    for col in range(COLS):
        rows = jnp.concatenate(
            [all_ref[tile, pl.ds(col, SLABS, stride=COLS), :] for tile in range(CHUNK // 128)], axis=1
        )
        for cell in range(PATCH_Z):
            grid_ref[cell * SLABS : (cell + 1) * SLABS, col * PATCH_Y : (col + 1) * PATCH_Y] = rows[
                :, cell * PATCH_Y : (cell + 1) * PATCH_Y
            ]
    by_y = dot3(split(grid_ref[...]), (y_h[...], y_l[...]))
    spectrum = dot3((z_h[...], z_l[...]), split(by_y))
    unit = 2.0 * math.pi / MESH
    index_z = lax.broadcasted_iota(jnp.int32, (MESH, MESH), 0)
    index_y = lax.broadcasted_iota(jnp.int32, (MESH, MESH), 1)
    index_x = jnp.full((MESH, MESH), index_ref[0, 0], jnp.int32)

    def square_of(index):
        wave = jnp.minimum(index, MESH - index).astype(F32) * unit
        return wave * wave

    square = square_of(index_z) + square_of(index_y) + square_of(index_x)
    nonzero = square > 0.0
    safe = jnp.where(nonzero, square, 1.0)
    green = jnp.where(nonzero, 4.0 * math.pi * jnp.exp(-0.5 * SMEAR * SMEAR * square) / safe, 0.0)
    filtered = spectrum * green
    energy = 0.5 * COUPLING * jnp.sum(spectrum * filtered, axis=(0, 1), keepdims=True)
    energy = energy + short_ref[0:1, 0:1]
    back_z = dot3((zt_h[...], zt_l[...]), split(filtered))
    grid_ref[...] = dot3(split(back_z), (yt_h[...], yt_l[...]))
    tail = jnp.broadcast_to(energy, (SLABS, CHUNK - PATCH))
    for col in range(COLS):
        pieces = [
            grid_ref[cell * SLABS : (cell + 1) * SLABS, col * PATCH_Y : (col + 1) * PATCH_Y]
            for cell in range(PATCH_Z)
        ]
        rows = jnp.concatenate(pieces + [tail], axis=1)
        for tile in range(CHUNK // 128):
            all_ref[tile, pl.ds(col, SLABS, stride=COLS), :] = rows[:, tile * 128 : (tile + 1) * 128]
    for tile in range(CHUNK // 128):
        out_ref[:, 0, tile * 128 : (tile + 1) * 128] = all_ref[tile]


def interpolate_kernel(
    back_ref,
    pos_ref,
    type_ref,
    count_ref,
    owner_ref,
    shift_ref,
    basis_h,
    basis_l,
    energy_ref,
    atom_ref,
    centre_ref,
    place_ref,
    all_ref,
):
    charge, owner = points(pos_ref, type_ref, count_ref, owner_ref, shift_ref, place_ref)
    basis = (basis_h[...], basis_l[...])
    along_x, slope_x = spline(wrapped(offsets(place_ref[0:1, :], MESH, 0)), True)
    along_y, slope_y = spline(offsets(place_ref[1:2, :], PATCH_Y, -REACH), True)
    along_z, slope_z = spline(offsets(place_ref[2:3, :], 16, -REACH), True)
    all_ref[...] = back_ref[:, 0, :]
    energy_ref[...] = jnp.broadcast_to(
        jnp.sum(all_ref[:, PATCH : PATCH + 1], axis=(0, 1), keepdims=True)
        * (1.0 / (ATOMS * SLABS * COLS)),
        (1, 128),
    )
    turned = split(jnp.transpose(all_ref[...]))
    values = dot3(turned, split(dot3(basis, split(along_x))))
    slopes = dot3(turned, split(dot3(basis, split(slope_x))))
    by_x = jnp.zeros((PATCH_Y, 256), F32)
    by_y = jnp.zeros((PATCH_Y, 256), F32)
    by_z = jnp.zeros((PATCH_Y, 256), F32)
    for cell in range(PATCH_Z):
        part = values[cell * PATCH_Y : (cell + 1) * PATCH_Y, :]
        by_x = by_x + along_z[cell : cell + 1, :] * slopes[cell * PATCH_Y : (cell + 1) * PATCH_Y, :]
        by_y = by_y + along_z[cell : cell + 1, :] * part
        by_z = by_z + slope_z[cell : cell + 1, :] * part
    scale = -COUPLING * charge
    force_x = jnp.sum(along_y * by_x, axis=0, keepdims=True) * scale
    force_y = jnp.sum(slope_y * by_y, axis=0, keepdims=True) * scale
    force_z = jnp.sum(along_y * by_z, axis=0, keepdims=True) * scale
    row = lax.broadcasted_iota(jnp.int32, (8, 256), 0)
    force = jnp.where(
        row == 0, force_x, jnp.where(row == 1, force_y, jnp.where(row == 2, force_z, 0.0))
    )
    atom_index = lax.broadcasted_iota(jnp.int32, (128, 128), 0)
    picker = jnp.where(atom_index == owner, 1.0, 0.0).astype(BF16)
    centre = force[:, 128:256]
    high, low = split(centre)
    lower = (centre - high.astype(F32) - low.astype(F32)).astype(BF16)
    dims = ((1,), (1,))
    carried = dot(high, picker, dims) + (dot(low, picker, dims) + dot(lower, picker, dims))
    atom_ref[...] = force[0:3, 0:128] + carried[0:3]
    centre_ref[...] = force[0:3, 128:160]


def column_of(row, scratch):
    n = row.shape[1]
    scratch[...] = jnp.zeros((128, 256), F32)
    scratch[:, 0:n] = jnp.broadcast_to(row, (128, n))
    return jnp.transpose(scratch[...])


def short_kernel(
    table_ref,
    type_ref,
    count_ref,
    mid_ref,
    low_ref,
    high_ref,
    emb1_ref,
    emb2_ref,
    bias2_ref,
    emb3_ref,
    bias3_ref,
    fit1_ref,
    fit_type_ref,
    fit2_ref,
    fit_bias_ref,
    fit_out_ref,
    energy_ref,
    own_ref,
    out_mid,
    out_low,
    out_high,
    turn_ref,
    flip_ref,
    index_ref,
    pair_ref,
    env_ref,
    first_ref,
    second_ref,
    third_ref,
    bias2_s,
    bias3_s,
    in2_ref,
    in3_ref,
    feat_ref,
    tang_ref,
    mom_ref,
    desc_ref,
    grad_mom_ref,
    den_ref,
    left_ref,
    pick_ref,
):
    ghost_refs = (low_ref, mid_ref, high_ref)
    turn_ref[...] = jnp.full((128, 128), -1.0, F32)
    turn_ref[:, 0:SLOTS] = table_ref[...].astype(F32)
    index_ref[...] = jnp.transpose(turn_ref[...])[0:SLOTS, :].astype(jnp.int32)
    centre = [mid_ref[1, c : c + 1, :] for c in range(3)]

    for group in range(SLOTS // 8):
        rows = slice(group * 8, group * 8 + 8)
        entry = index_ref[rows, :]
        live = jnp.where(entry >= 0, 1.0, 0.0)
        entry = jnp.maximum(entry, 0)
        block = entry // ATOMS
        atom = entry % ATOMS
        near = [jnp.zeros((8, 128), F32) for _ in range(4)]
        for b in range(9):
            ghost = ghost_refs[b % 3]
            here = block == b
            for c in range(4):
                line = ghost[b // 3, c : c + 1, :]
                if c == 1:
                    line = line + float((b % 3 - 1) * CELL_Y)
                if c == 2:
                    line = line + float((b // 3 - 1) * CELL_Z)
                near[c] = jnp.where(here, lanes(jnp.broadcast_to(line, (8, 128)), atom), near[c])
        v = [(near[c] - centre[c]) * (1.0 / RANGE) for c in range(3)]
        inverse = 1.0 / jnp.sqrt(1.0 + (v[0] * v[0] + v[1] * v[1] + v[2] * v[2]))
        for c in range(3):
            pair_ref[c, rows, :] = v[c]
            env_ref[c + 1, rows, :] = live * v[c] * inverse * inverse
        pair_ref[3, rows, :] = near[3]
        pair_ref[4, rows, :] = inverse
        pair_ref[5, rows, :] = live
        env_ref[0, rows, :] = live * inverse

    first_ref[...] = jnp.zeros((5, 32, 128), F32)
    for c in range(5):
        first_ref[c, 0:25, :] = jnp.broadcast_to(emb1_ref[:, c : c + 1], (25, 128))
    second_ref[...] = jnp.zeros((64, 128), F32)
    third_ref[...] = jnp.zeros((128, 256), F32)
    for half in range(2):
        block = emb2_ref[half * 25 : half * 25 + 25, :]
        high = block.astype(BF16).astype(F32)
        for stack, part in enumerate((high, high, block - high)):
            second_ref[half * 32 : half * 32 + 25, stack * 32 : stack * 32 + 25] = part
    for quarter in range(4):
        for half in range(2):
            block = emb3_ref[quarter * 25 : quarter * 25 + 25, half * 25 : half * 25 + 25]
            high = block.astype(BF16).astype(F32)
            for stack, part in enumerate((high, high, block - high)):
                start = stack * 64 + half * 32
                third_ref[quarter * 32 : quarter * 32 + 25, start : start + 25] = part
    bias = column_of(bias2_ref[...], flip_ref)
    bias2_s[...] = jnp.zeros((64, 128), F32)
    for half in range(2):
        bias2_s[half * 32 : half * 32 + 25, :] = bias[half * 25 : half * 25 + 25, :]
    bias = column_of(bias3_ref[...], flip_ref)
    bias3_s[...] = jnp.zeros((128, 128), F32)
    for quarter in range(4):
        bias3_s[quarter * 32 : quarter * 32 + 25, :] = bias[quarter * 25 : quarter * 25 + 25, :]
    weight2 = second_ref[:, 0:96].astype(BF16)
    weight3 = third_ref[:, 0:192].astype(BF16)
    mom_ref[...] = jnp.zeros((4, 128, 128), F32)
    half_lanes = GROUP * 128

    def forward(group, carry):
        base = pl.multiple_of(group * GROUP, GROUP)
        smooth = env_ref[0, pl.ds(base, GROUP), :]
        kinds = pair_ref[3, pl.ds(base, GROUP), :]
        slope_row = first_ref[0]
        one, d_one = [], []
        for j in range(GROUP):
            s = smooth[j : j + 1, :]
            kind = kinds[j : j + 1, :]
            term = jnp.where(
                kind == 0.0,
                first_ref[1],
                jnp.where(kind == 1.0, first_ref[2], jnp.where(kind == 2.0, first_ref[3], first_ref[4])),
            )
            x = jnp.tanh(slope_row * s + term)
            d = (1.0 - x * x) * slope_row
            for value, start in ((x, j * 128), (d, half_lanes + j * 128)):
                high, low = split(value)
                in2_ref[0:32, start : start + 128] = high
                in2_ref[32:64, start : start + 128] = low
                in2_ref[64:96, start : start + 128] = high
            one.append(x)
            d_one.append(d)
        pre = dot(weight2, in2_ref[...])
        two, d_two = [], []
        for j in range(GROUP):
            h = jnp.tanh(pre[:, j * 128 : (j + 1) * 128] + bias2_s[...])
            x = h + jnp.concatenate([one[j], one[j]], axis=0)
            d = (1.0 - h * h) * pre[
                :, half_lanes + j * 128 : half_lanes + (j + 1) * 128
            ] + jnp.concatenate([d_one[j], d_one[j]], axis=0)
            for value, start in ((x, j * 128), (d, half_lanes + j * 128)):
                high, low = split(value)
                in3_ref[0:64, start : start + 128] = high
                in3_ref[64:128, start : start + 128] = low
                in3_ref[128:192, start : start + 128] = high
            two.append(x)
            d_two.append(d)
        pre = dot(weight3, in3_ref[...])
        for j in range(GROUP):
            h = jnp.tanh(pre[:, j * 128 : (j + 1) * 128] + bias3_s[...])
            feat_ref[base + j] = h + jnp.concatenate([two[j], two[j]], axis=0)
            tang_ref[base + j] = (1.0 - h * h) * pre[
                :, half_lanes + j * 128 : half_lanes + (j + 1) * 128
            ] + jnp.concatenate([d_two[j], d_two[j]], axis=0)
        envelope = [env_ref[c, pl.ds(base, GROUP), :] for c in range(4)]
        for block in range(16):
            rows = slice(block * 8, block * 8 + 8)
            total = [mom_ref[c, rows, :] for c in range(4)]
            for j in range(GROUP):
                x = feat_ref[base + j, rows, :]
                for c in range(4):
                    total[c] = total[c] + envelope[c][j : j + 1, :] * x
            for c in range(4):
                mom_ref[c, rows, :] = total[c]
        return carry

    lax.fori_loop(0, SLOTS // GROUP, forward, 0)
    mom_ref[...] = mom_ref[...] * (1.0 / SLOTS)

    lead = [mom_ref[c, 0:16, :] for c in range(4)]
    for m in range(100):
        r = m // 25 * 32 + m % 25
        total = mom_ref[0, r : r + 1, :] * lead[0]
        for c in range(1, 4):
            total = total + mom_ref[c, r : r + 1, :] * lead[c]
        desc_ref[m * 16 : m * 16 + 16, :] = total

    weight = split(fit1_ref[...])
    hidden = dot3(weight, split(desc_ref[...]))
    kind = type_ref[...]
    term = jnp.where(
        kind == 0,
        fit_type_ref[:, 0:1],
        jnp.where(kind == 1, fit_type_ref[:, 1:2], jnp.where(kind == 2, fit_type_ref[:, 2:3], fit_type_ref[:, 3:4])),
    )
    first = jnp.tanh(hidden + term)
    weight_2 = split(fit2_ref[...])
    bias = column_of(fit_bias_ref[...], flip_ref)[0:240, :]
    second = jnp.tanh(dot3(weight_2, split(first)) + bias)
    lane = lax.broadcasted_iota(jnp.int32, (1, 128), 1)
    own_live = jnp.where(lane < count_ref[0, 0], 1.0, 0.0)
    read = column_of(fit_out_ref[...], flip_ref)[0:240, :]
    energy = jnp.sum(read * (first + second) * own_live, axis=(0, 1), keepdims=True)
    energy_ref[...] = jnp.broadcast_to(energy, (8, 128))
    upper = read * own_live
    inner = upper * (1.0 - second * second)
    back = upper + dot3(weight_2, split(inner), ((0,), (0,)))
    back = back * (1.0 - first * first)
    flip_ref[...] = jnp.zeros((128, 256), F32)
    flip_ref[:, 0:240] = jnp.transpose(back)
    turned = dot3(split(flip_ref[:, 0:240]), weight)
    for part in range(12):
        desc_ref[part * 128 : (part + 1) * 128, :] = jnp.transpose(turned[:, part * 128 : (part + 1) * 128])
    desc_ref[1536:1600, :] = jnp.transpose(turned[:, 1536:1600])

    grad_mom_ref[...] = jnp.zeros((4, 128, 128), F32)
    gathered = [jnp.zeros((16, 128), F32) for _ in range(4)]
    for m in range(100):
        r = m // 25 * 32 + m % 25
        part = desc_ref[m * 16 : m * 16 + 16, :]
        for c in range(4):
            gathered[c] = gathered[c] + mom_ref[c, r : r + 1, :] * part
            grad_mom_ref[c, r : r + 1, :] = jnp.sum(part * lead[c], axis=0, keepdims=True)
    for c in range(4):
        grad_mom_ref[c, 0:16, :] = grad_mom_ref[c, 0:16, :] + gathered[c]
    grad_mom_ref[...] = grad_mom_ref[...] * (1.0 / SLOTS)

    step = 4

    def backward(group, carry):
        base = pl.multiple_of(group * step, step)
        value = [[jnp.zeros((8, 128), F32) for _ in range(4)] for _ in range(step)]
        slope = [[jnp.zeros((8, 128), F32) for _ in range(4)] for _ in range(step)]
        for block in range(16):
            rows = slice(block * 8, block * 8 + 8)
            grads = [grad_mom_ref[c, rows, :] for c in range(4)]
            for j in range(step):
                x = feat_ref[base + j, rows, :]
                d = tang_ref[base + j, rows, :]
                for c in range(4):
                    value[j][c] = value[j][c] + grads[c] * x
                    slope[j][c] = slope[j][c] + grads[c] * d
        for j in range(step):
            through = jnp.zeros((8, 128), F32)
            for c in range(4):
                through = through + env_ref[c, pl.ds(base + j, 1), :] * slope[j][c]
                den_ref[c, pl.ds(base + j, 1), :] = jnp.sum(value[j][c], axis=0, keepdims=True)
            den_ref[4, pl.ds(base + j, 1), :] = jnp.sum(through, axis=0, keepdims=True)
        return carry

    lax.fori_loop(0, SLOTS // step, backward, 0)

    own = [jnp.zeros((8, 128), F32) for _ in range(3)]
    for group in range(SLOTS // 8):
        rows = slice(group * 8, group * 8 + 8)
        v = [pair_ref[c, rows, :] for c in range(3)]
        inverse = pair_ref[4, rows, :]
        scale = pair_ref[5, rows, :] * inverse * inverse * (1.0 / RANGE)
        by_v = [den_ref[c + 1, rows, :] for c in range(3)]
        along = v[0] * by_v[0] + v[1] * by_v[1] + v[2] * by_v[2]
        radial = inverse * (den_ref[0, rows, :] + den_ref[4, rows, :] + 2.0 * inverse * along)
        for c in range(3):
            grad = scale * (by_v[c] - v[c] * radial)
            pair_ref[c, rows, :] = grad
            own[c] = own[c] - grad
    row8 = lax.broadcasted_iota(jnp.int32, (8, 128), 0)
    own_rows = [jnp.sum(own[c], axis=0, keepdims=True) for c in range(3)]
    own_ref[...] = jnp.where(
        row8[0:4] == 0, own_rows[0], jnp.where(row8[0:4] == 1, own_rows[1], jnp.where(row8[0:4] == 2, own_rows[2], 0.0))
    )

    line = lax.broadcasted_iota(jnp.int32, (48, 128), 0)
    direction = line % 4
    domain = line // 12 + 3 * (line // 4 % 3)
    domain = jnp.where(line < 36, domain, -1)
    atom_index = lax.broadcasted_iota(jnp.int32, (128, 128), 0)

    def scatter(group, total):
        base = pl.multiple_of(group * GROUP, GROUP)
        entry = jnp.maximum(index_ref[pl.ds(base, GROUP), :], 0)
        block = entry // ATOMS
        atom = entry % ATOMS
        grads = [pair_ref[c, pl.ds(base, GROUP), :] for c in range(3)]
        for j in range(GROUP):
            grad = jnp.where(
                direction == 0,
                grads[0][j : j + 1, :],
                jnp.where(direction == 1, grads[1][j : j + 1, :], grads[2][j : j + 1, :]),
            )
            grad = jnp.where((domain == block[j : j + 1, :]) & (direction < 3), grad, 0.0)
            high, low = split(grad)
            left_ref[0:48, j * 128 : (j + 1) * 128] = high
            left_ref[48:96, j * 128 : (j + 1) * 128] = low
            pick_ref[:, j * 128 : (j + 1) * 128] = jnp.where(atom_index == atom[j : j + 1, :], 1.0, 0.0).astype(BF16)
        return total + dot(left_ref[...], pick_ref[...], ((1,), (1,)))

    total = lax.fori_loop(0, SLOTS // GROUP, scatter, jnp.zeros((96, 128), F32))
    total = total[0:48] + total[48:96]
    for col, out in enumerate((out_low, out_mid, out_high)):
        for slab in range(3):
            start = col * 12 + slab * 4
            out[slab] = total[start : start + 4]


def call(kernel, outs, scratch, operands, name, flops, moved, smem=()):
    vmem = pl.BlockSpec(memory_space=pltpu.VMEM)
    scalar = pl.BlockSpec(memory_space=pltpu.SMEM)
    return pl.pallas_call(
        kernel,
        out_shape=[jax.ShapeDtypeStruct(shape, F32) for shape in outs],
        in_specs=[scalar if i in smem else vmem for i in range(len(operands))],
        out_specs=[vmem] * len(outs),
        scratch_shapes=[pltpu.VMEM(shape, dtype) for shape, dtype in scratch],
        name=name,
        cost_estimate=pl.CostEstimate(flops=flops, bytes_accessed=moved, transcendentals=0),
        compiler_params=pltpu.CompilerParams(vmem_limit_bytes=40 * 2**20),
    )(*operands)


def local(
    positions,
    atom_types,
    atom_counts,
    neighbours,
    centroid_owner_atoms,
    centroid_cell_offsets,
    emb_first,
    emb_second,
    emb_second_bias,
    emb_third,
    emb_third_bias,
    fit_first,
    fit_type,
    fit_second,
    fit_second_bias,
    fit_out,
):
    basis_h, basis_l, z_h, z_l, zt_h, zt_l, y_h, y_l, yt_h, yt_l = tables()
    pos = positions.reshape(3, ATOMS)
    kinds = atom_types.reshape(1, ATOMS)
    count = atom_counts.reshape(1, 1)
    owner = centroid_owner_atoms.reshape(1, CENTRES)
    shift = centroid_cell_offsets.reshape(3, CENTRES)
    index = (lax.axis_index("slab") * COLS + lax.axis_index("col")).reshape(1, 1)

    def ring(value, axis, step):
        size = lax.axis_size(axis)
        return lax.ppermute(value, axis, [(i, (i + step) % size) for i in range(size)])

    extent = jnp.array([[MESH], [CELL_Y], [CELL_Z]], F32)
    packed = jnp.concatenate([pos * extent, kinds.astype(F32)], 0)[None]
    mid = jnp.concatenate([ring(packed, "slab", 1), packed, ring(packed, "slab", -1)], 0)
    low = ring(mid, "col", 1)
    high = ring(mid, "col", -1)

    (outgoing,) = call(
        spread_kernel,
        [(MESH, 1, CHUNK)],
        [((8, 256), F32), ((PATCH, 256), F32), ((PATCH, 256), F32), ((MESH, CHUNK), F32)],
        [pos, kinds, count, owner, shift, basis_h, basis_l],
        "spread",
        400_000_000,
        1_000_000,
        (2,),
    )
    plane = lax.all_to_all(outgoing, BOTH, 0, 0, tiled=True)

    pairs = SLOTS * ATOMS
    short, own, back_mid, back_low, back_high = call(
        short_kernel,
        [(8, 128), (4, 128), (3, 4, 128), (3, 4, 128), (3, 4, 128)],
        [
            ((128, 128), F32),
            ((128, 256), F32),
            ((SLOTS, 128), jnp.int32),
            ((6, SLOTS, 128), F32),
            ((4, SLOTS, 128), F32),
            ((5, 32, 128), F32),
            ((64, 128), F32),
            ((128, 256), F32),
            ((64, 128), F32),
            ((128, 128), F32),
            ((96, 2 * GROUP * 128), BF16),
            ((192, 2 * GROUP * 128), BF16),
            ((SLOTS, 128, 128), F32),
            ((SLOTS, 128, 128), F32),
            ((4, 128, 128), F32),
            ((1600, 128), F32),
            ((4, 128, 128), F32),
            ((5, SLOTS, 128), F32),
            ((96, GROUP * 128), BF16),
            ((128, GROUP * 128), BF16),
        ],
        [
            neighbours.reshape(ATOMS, SLOTS),
            kinds,
            count,
            mid,
            low,
            high,
            emb_first,
            emb_second,
            emb_second_bias.reshape(1, -1),
            emb_third,
            emb_third_bias.reshape(1, -1),
            fit_first,
            fit_type,
            fit_second,
            fit_second_bias.reshape(1, -1),
            fit_out.reshape(1, -1),
        ],
        "short",
        pairs * 400_000,
        4_000_000,
        (2,),
    )

    (returning,) = call(
        solve_kernel,
        [(MESH, 1, CHUNK)],
        [((CHUNK // 128, MESH, 128), F32), ((PATCH_Z * SLABS, PATCH_Y * COLS), F32)],
        [plane, short, index, z_h, z_l, zt_h, zt_l, y_h, y_l, yt_h, yt_l],
        "solve",
        400_000_000,
        2_000_000,
        (2,),
    )
    potential = lax.all_to_all(returning, BOTH, 0, 0, tiled=True)

    ghosts = back_mid + ring(back_low, "col", -1) + ring(back_high, "col", 1)
    ghosts = ghosts[1] + ring(ghosts[0], "slab", -1) + ring(ghosts[2], "slab", 1)

    energy, atom_force, centre_force = call(
        interpolate_kernel,
        [(1, 128), (3, ATOMS), (3, CENTRES)],
        [((8, 256), F32), ((MESH, CHUNK), F32)],
        [potential, pos, kinds, count, owner, shift, basis_h, basis_l],
        "interpolate",
        600_000_000,
        1_500_000,
        (3,),
    )
    forces = atom_force - (own + ghosts)[0:3]
    return energy[0, 0], forces[None, None], centre_force[None, None]


def solution(mesh):
    return jax.shard_map(
        local,
        mesh=mesh,
        in_specs=(
            P("slab", "col", None, None),
            P("slab", "col", None),
            P("slab", "col"),
            P("slab", "col", None, None),
            P("slab", "col", None),
            P("slab", "col", None, None),
            P(),
            P(),
            P(),
            P(),
            P(),
            P(),
            P(),
            P(),
            P(),
            P(),
        ),
        out_specs=(P(), P("slab", "col", None, None), P("slab", "col", None, None)),
        check_vma=False,
    )
```

```python
import functools
import math

import jax
import jax.numpy as jnp
import ml_dtypes
import numpy as np
from jax import lax
from jax.experimental import pallas as pl
from jax.experimental.pallas import tpu as pltpu
from jax.sharding import PartitionSpec as P

CHARGES = (6.0, 1.0, 1.0, -1.0)
WANNIER = -8.0
RANGE = 24.0
COUPLING = 0.05
SMEAR = 0.6
ATOMS = 128
CENTRES = 32
SLOTS = 64
MESH = 256
SLABS, COLS = 32, 8
CELL_Z, CELL_Y = 8, 32
REACH = 3
PATCH_Z, PATCH_Y = 14, 40
PATCH = PATCH_Z * PATCH_Y
CHUNK_IN = 384
CHUNK = 640
GROUP = 16
F32 = jnp.float32
BF16 = jnp.bfloat16
BOTH = ("slab", "col")


def halves(array):
    high = array.astype(ml_dtypes.bfloat16)
    low = (array - high.astype(np.float64)).astype(ml_dtypes.bfloat16)
    return high, low


@functools.lru_cache(maxsize=None)
def tables():
    k = np.arange(MESH)[:, None]
    n = np.arange(MESH)[None, :]
    phase = 2.0 * np.pi * ((k * n) % MESH) / MESH
    basis = np.where(k <= MESH // 2, np.cos(phase), np.sin(phase)) * math.sqrt(2.0 / MESH)
    basis[0] = 1.0 / math.sqrt(MESH)
    basis[MESH // 2] = np.where(np.arange(MESH) % 2 == 0, 1.0, -1.0) / math.sqrt(MESH)
    cells_z = (np.arange(PATCH_Z)[:, None] - REACH + CELL_Z * np.arange(SLABS)[None, :]) % MESH
    along_z = basis[:, cells_z.reshape(-1)]
    cells_z = (np.arange(CELL_Z)[:, None] + CELL_Z * np.arange(SLABS)[None, :]) % MESH
    inside_z = basis[:, cells_z.reshape(-1)]
    cells_y = (np.arange(PATCH_Y)[None, :] - REACH + CELL_Y * np.arange(COLS)[:, None]) % MESH
    along_y = basis[:, cells_y.reshape(-1)].T
    out = []
    for matrix in (basis, inside_z, along_z.T, along_y, along_y.T):
        out.extend(halves(matrix))
    return out


def split(value):
    high = value.astype(BF16)
    return high, (value - high.astype(F32)).astype(BF16)


def dot(left, right, dims=((1,), (0,))):
    return lax.dot_general(left, right, (dims, ((), ())), preferred_element_type=F32)


def dot3(left, right, dims=((1,), (0,))):
    return dot(left[0], right[0], dims) + (dot(left[0], right[1], dims) + dot(left[1], right[0], dims))


def lanes(table, index):
    return jnp.take_along_axis(table, index, axis=1)


def spline(z, slope):
    a = jnp.abs(z)
    a2 = z * z
    rest = 2.5 - a
    rest2 = rest * rest
    inner = 115.0 / 192.0 + a2 * (-0.625 + 0.25 * a2)
    middle = (55.0 + a * (20.0 + a * (-120.0 + a * (80.0 - 16.0 * a)))) * (1.0 / 96.0)
    outer = rest2 * rest2 * (1.0 / 24.0)
    near, mid, far = a < 0.5, a < 1.5, a < 2.5
    value = jnp.where(near, inner, jnp.where(mid, middle, jnp.where(far, outer, 0.0)))
    if not slope:
        return value, None
    d_inner = a * (a2 - 1.25)
    d_middle = (20.0 + a * (-240.0 + a * (240.0 - 64.0 * a))) * (1.0 / 96.0)
    d_outer = rest2 * rest * (-1.0 / 6.0)
    d = jnp.where(near, d_inner, jnp.where(mid, d_middle, jnp.where(far, d_outer, 0.0)))
    return value, jnp.where(z < 0.0, -d, d)


def points(pos_ref, type_ref, count_ref, owner_ref, shift_ref, place_ref):
    lane = lax.broadcasted_iota(jnp.int32, (8, 128), 1)
    place_ref[...] = jnp.zeros((8, 256), F32)
    place_ref[0:3, 0:128] = pos_ref[:, 0, :]
    place_ref[0:3, 128:160] = shift_ref[:, 0, :]
    place_ref[3:4, 128:160] = owner_ref[...].astype(F32)
    row = lax.broadcasted_iota(jnp.int32, (8, 128), 0)
    extent = jnp.where(row == 0, float(MESH), jnp.where(row == 1, float(CELL_Y), float(CELL_Z)))
    atoms = place_ref[:, 0:128] * extent
    owner = jnp.where(lane < CENTRES, place_ref[3:4, 128:256].astype(jnp.int32), -1)
    carrying = jnp.broadcast_to(jnp.maximum(owner, 0), (8, 128))
    centres = lanes(atoms, carrying) + place_ref[:, 128:256]
    kind = type_ref[...]
    charge = jnp.where(
        kind == 0, CHARGES[0], jnp.where(kind == 1, CHARGES[1], jnp.where(kind == 2, CHARGES[2], CHARGES[3]))
    )
    charge = jnp.where(lane[0:1] < count_ref[0, 0], charge, 0.0)
    centre_charge = jnp.where(owner[0:1] >= 0, WANNIER, 0.0)
    place_ref[:, 0:128] = atoms
    place_ref[:, 128:256] = centres
    return jnp.concatenate([charge, centre_charge], axis=1), owner[0:1]


def offsets(coordinate, cells, low):
    cell = lax.broadcasted_iota(jnp.int32, (cells, coordinate.shape[1]), 0) + low
    return coordinate - cell.astype(F32) - 0.5


def wrapped(z):
    return z - float(MESH) * jnp.round(z * (1.0 / MESH))


def pack_kernel(*refs):
    sources, (count_ref, out_ref, place_ref), copies, sems = refs[:4], refs[4:7], refs[7:11], refs[11]
    moves = [pltpu.make_async_copy(a, b, sems.at[i]) for i, (a, b) in enumerate(zip(sources, copies))]
    for move in moves:
        move.start()
    for move in moves:
        move.wait()
    pos_ref, type_ref, owner_ref, shift_ref = copies
    charge, _ = points(pos_ref, type_ref, count_ref, owner_ref, shift_ref, place_ref)
    out_ref[0] = jnp.zeros((8, 128), F32)
    out_ref[0, 0:3, :] = place_ref[0:3, 0:128]
    out_ref[0, 3:4, :] = type_ref[...].astype(F32)
    out_ref[0, 4:5, :] = charge[:, 0:128]
    for c in range(3):
        out_ref[0, 5:6, c * 32 : c * 32 + 32] = place_ref[c : c + 1, 128:160]
    out_ref[0, 5:6, 96:128] = charge[:, 128:160]


def spread_kernel(mid_ref, basis_h, basis_l, out_ref, place_ref, amp_h, amp_l, all_ref):
    place_ref[...] = jnp.zeros((8, 512), F32)
    for d in range(3):
        shift = (0.0, 0.0, float((d - 1) * CELL_Z), 0.0)
        for c, row in enumerate((0, 1, 2, 4)):
            place_ref[c : c + 1, d * 128 : d * 128 + 128] = mid_ref[d, row : row + 1, :] + shift[c]
            place_ref[c : c + 1, 384 + d * 32 : 416 + d * 32] = mid_ref[d, 5:6, c * 32 : c * 32 + 32] + shift[c]
    along_x, _ = spline(wrapped(offsets(place_ref[0:1, :], MESH, 0)), False)
    along_y, _ = spline(offsets(place_ref[1:2, :], PATCH_Y, -REACH), False)
    along_z, _ = spline(offsets(place_ref[2:3, :], CELL_Z, 0), False)
    along_z = along_z * place_ref[3:4, :]
    for cell in range(CELL_Z):
        block = along_z[cell : cell + 1, :] * along_y
        high = block.astype(BF16).astype(F32)
        amp_h[cell * PATCH_Y : (cell + 1) * PATCH_Y, :] = high
        amp_l[cell * PATCH_Y : (cell + 1) * PATCH_Y, :] = block - high
    spectral = split(dot3((basis_h[...], basis_l[...]), split(along_x)))
    all_ref[...] = jnp.zeros((MESH, CHUNK_IN), F32)
    all_ref[:, 0 : CELL_Z * PATCH_Y] = dot3(
        spectral, (amp_h[...].astype(BF16), amp_l[...].astype(BF16)), ((1,), (1,))
    )
    out_ref[:, 0, :] = all_ref[...]


def solve_kernel(
    plane_ref, short_ref, index_ref, z_h, z_l, zt_h, zt_l, y_h, y_l, yt_h, yt_l, out_ref, all_ref, grid_ref
):
    for tile in range(CHUNK_IN // 128):
        all_ref[tile] = plane_ref[:, 0, tile * 128 : (tile + 1) * 128]
    for col in range(COLS):
        rows = jnp.concatenate(
            [all_ref[tile, pl.ds(col, SLABS, stride=COLS), :] for tile in range(CHUNK_IN // 128)], axis=1
        )
        for cell in range(CELL_Z):
            grid_ref[cell * SLABS : (cell + 1) * SLABS, col * PATCH_Y : (col + 1) * PATCH_Y] = rows[
                :, cell * PATCH_Y : (cell + 1) * PATCH_Y
            ]
    by_y = dot3(split(grid_ref[0 : CELL_Z * SLABS, :]), (y_h[...], y_l[...]))
    spectrum = dot3((z_h[...], z_l[...]), split(by_y))
    unit = 2.0 * math.pi / MESH
    index_z = lax.broadcasted_iota(jnp.int32, (MESH, MESH), 0)
    index_y = lax.broadcasted_iota(jnp.int32, (MESH, MESH), 1)
    index_x = jnp.full((MESH, MESH), index_ref[0, 0], jnp.int32)

    def square_of(index):
        wave = jnp.minimum(index, MESH - index).astype(F32) * unit
        return wave * wave

    square = square_of(index_z) + square_of(index_y) + square_of(index_x)
    nonzero = square > 0.0
    safe = jnp.where(nonzero, square, 1.0)
    green = jnp.where(nonzero, 4.0 * math.pi * jnp.exp(-0.5 * SMEAR * SMEAR * square) / safe, 0.0)
    filtered = spectrum * green
    energy = 0.5 * COUPLING * jnp.sum(spectrum * filtered, axis=(0, 1), keepdims=True)
    energy = energy + short_ref[0:1, 0:1]
    back_z = dot3((zt_h[...], zt_l[...]), split(filtered))
    grid_ref[...] = dot3(split(back_z), (yt_h[...], yt_l[...]))
    tail = jnp.broadcast_to(energy, (SLABS, CHUNK - PATCH))
    for col in range(COLS):
        pieces = [
            grid_ref[cell * SLABS : (cell + 1) * SLABS, col * PATCH_Y : (col + 1) * PATCH_Y]
            for cell in range(PATCH_Z)
        ]
        rows = jnp.concatenate(pieces + [tail], axis=1)
        for tile in range(CHUNK // 128):
            all_ref[tile, pl.ds(col, SLABS, stride=COLS), :] = rows[:, tile * 128 : (tile + 1) * 128]
    for tile in range(CHUNK // 128):
        out_ref[:, 0, tile * 128 : (tile + 1) * 128] = all_ref[tile]


def interpolate_kernel(
    back_ref,
    pos_ref,
    type_ref,
    count_ref,
    owner_ref,
    shift_ref,
    basis_h,
    basis_l,
    own_ref,
    kept_ref,
    from_low,
    from_high,
    energy_ref,
    atom_ref,
    centre_ref,
    place_ref,
    all_ref,
):
    charge, owner = points(pos_ref, type_ref, count_ref, owner_ref, shift_ref, place_ref)
    basis = (basis_h[...], basis_l[...])
    along_x, slope_x = spline(wrapped(offsets(place_ref[0:1, :], MESH, 0)), True)
    along_y, slope_y = spline(offsets(place_ref[1:2, :], PATCH_Y, -REACH), True)
    along_z, slope_z = spline(offsets(place_ref[2:3, :], 16, -REACH), True)
    all_ref[...] = back_ref[:, 0, :]
    energy_ref[...] = jnp.broadcast_to(
        jnp.sum(all_ref[:, PATCH : PATCH + 1], axis=(0, 1), keepdims=True)
        * (1.0 / (ATOMS * SLABS * COLS)),
        (1, 128),
    )
    turned = split(jnp.transpose(all_ref[...]))
    values = dot3(turned, split(dot3(basis, split(along_x))))
    slopes = dot3(turned, split(dot3(basis, split(slope_x))))
    by_x = jnp.zeros((PATCH_Y, 256), F32)
    by_y = jnp.zeros((PATCH_Y, 256), F32)
    by_z = jnp.zeros((PATCH_Y, 256), F32)
    for cell in range(PATCH_Z):
        part = values[cell * PATCH_Y : (cell + 1) * PATCH_Y, :]
        by_x = by_x + along_z[cell : cell + 1, :] * slopes[cell * PATCH_Y : (cell + 1) * PATCH_Y, :]
        by_y = by_y + along_z[cell : cell + 1, :] * part
        by_z = by_z + slope_z[cell : cell + 1, :] * part
    scale = -COUPLING * charge
    force_x = jnp.sum(along_y * by_x, axis=0, keepdims=True) * scale
    force_y = jnp.sum(slope_y * by_y, axis=0, keepdims=True) * scale
    force_z = jnp.sum(along_y * by_z, axis=0, keepdims=True) * scale
    row = lax.broadcasted_iota(jnp.int32, (8, 256), 0)
    force = jnp.where(
        row == 0, force_x, jnp.where(row == 1, force_y, jnp.where(row == 2, force_z, 0.0))
    )
    atom_index = lax.broadcasted_iota(jnp.int32, (128, 128), 0)
    picker = jnp.where(atom_index == owner, 1.0, 0.0).astype(BF16)
    centre = force[:, 128:256]
    high, low = split(centre)
    lower = (centre - high.astype(F32) - low.astype(F32)).astype(BF16)
    dims = ((1,), (1,))
    carried = dot(high, picker, dims) + (dot(low, picker, dims) + dot(lower, picker, dims))
    short = (own_ref[...] + kept_ref[1]) + (from_low[...] + from_high[...])
    atom_ref[:, 0, :] = force[0:3, 0:128] + carried[0:3] - short[0:3]
    centre_ref[:, 0, :] = force[0:3, 128:160]


def short_kernel(
    table_ref,
    type_ref,
    count_ref,
    mid_ref,
    low_ref,
    high_ref,
    emb1_ref,
    emb2_ref,
    bias2_ref,
    emb3_ref,
    bias3_ref,
    fit1_hbm,
    fit_type_ref,
    fit2_ref,
    fit_bias_ref,
    fit_out_ref,
    energy_ref,
    own_ref,
    out_mid,
    out_low,
    out_high,
    fit1_ref,
    fit1_sem,
    turn_ref,
    flip_ref,
    pair_ref,
    env_ref,
    first_ref,
    second_ref,
    third_ref,
    bias2_s,
    bias3_s,
    in2_ref,
    in3_ref,
    feat_ref,
    tang_ref,
    mom_ref,
    desc_ref,
    grad_mom_ref,
    den_ref,
    left_ref,
    pick_ref,
):
    ghost_refs = (low_ref, mid_ref, high_ref)
    fit1_copy = pltpu.make_async_copy(fit1_hbm, fit1_ref, fit1_sem)
    fit1_copy.start()
    centre = [mid_ref[1, c : c + 1, :] for c in range(3)]

    for group in range(SLOTS // 8):
        rows = slice(group * 8, group * 8 + 8)
        entry = table_ref[rows, :]
        live = jnp.where(entry >= 0, 1.0, 0.0)
        entry = jnp.maximum(entry, 0)
        block = entry // ATOMS
        atom = entry % ATOMS
        near = [jnp.zeros((8, 128), F32) for _ in range(4)]
        for b in range(9):
            ghost = ghost_refs[b % 3]
            here = block == b
            for c in range(4):
                line = ghost[b // 3, c : c + 1, :]
                if c == 1:
                    line = line + float((b % 3 - 1) * CELL_Y)
                if c == 2:
                    line = line + float((b // 3 - 1) * CELL_Z)
                near[c] = jnp.where(here, lanes(jnp.broadcast_to(line, (8, 128)), atom), near[c])
        v = [(near[c] - centre[c]) * (1.0 / RANGE) for c in range(3)]
        inverse = 1.0 / jnp.sqrt(1.0 + (v[0] * v[0] + v[1] * v[1] + v[2] * v[2]))
        for c in range(3):
            pair_ref[c, rows, :] = v[c]
            env_ref[c + 1, rows, :] = live * v[c] * inverse * inverse
        pair_ref[3, rows, :] = near[3]
        pair_ref[4, rows, :] = inverse
        pair_ref[5, rows, :] = live
        env_ref[0, rows, :] = live * inverse

    flip_ref[...] = jnp.zeros((128, 256), F32)
    flip_ref[0:5, 0:25] = emb1_ref[...]
    flip_ref[5:6, 0:50] = bias2_ref[...]
    flip_ref[6:7, 0:100] = bias3_ref[...]
    flip_ref[7:8, 0:240] = fit_bias_ref[...]
    flip_ref[8:9, 0:240] = fit_out_ref[...]
    flip_ref[9:13, 0:240] = fit_type_ref[...]
    turn_ref[...] = jnp.transpose(flip_ref[...])

    def column(at, start, stop):
        return jnp.broadcast_to(turn_ref[start:stop, at : at + 1], (stop - start, 128))

    first_ref[...] = jnp.zeros((5, 32, 128), F32)
    for c in range(5):
        first_ref[c, 0:25, :] = column(c, 0, 25)
    bias2_s[...] = jnp.zeros((64, 128), F32)
    for half in range(2):
        bias2_s[half * 32 : half * 32 + 25, :] = column(5, half * 25, half * 25 + 25)
    bias3_s[...] = jnp.zeros((128, 128), F32)
    for quarter in range(4):
        bias3_s[quarter * 32 : quarter * 32 + 25, :] = column(6, quarter * 25, quarter * 25 + 25)
    second_ref[...] = jnp.zeros((128, 128), F32)
    third_ref[...] = jnp.zeros((256, 128), F32)
    for half in range(2):
        block = emb2_ref[:, half * 25 : half * 25 + 25]
        high = block.astype(BF16).astype(F32)
        for stack, part in enumerate((high, high, block - high)):
            second_ref[stack * 32 : stack * 32 + 25, half * 32 : half * 32 + 25] = part
    for quarter in range(4):
        for half in range(2):
            block = emb3_ref[half * 25 : half * 25 + 25, quarter * 25 : quarter * 25 + 25]
            high = block.astype(BF16).astype(F32)
            for stack, part in enumerate((high, high, block - high)):
                start = stack * 64 + half * 32
                third_ref[start : start + 25, quarter * 32 : quarter * 32 + 25] = part
    weight2 = jnp.transpose(second_ref[...])[0:64, 0:96].astype(BF16)
    weight3 = jnp.transpose(third_ref[...])[:, 0:192].astype(BF16)
    mom_ref[...] = jnp.zeros((4, 128, 128), F32)
    half_lanes = GROUP * 128

    def forward(group, carry):
        base = pl.multiple_of(group * GROUP, GROUP)
        smooth = env_ref[0, pl.ds(base, GROUP), :]
        kinds = pair_ref[3, pl.ds(base, GROUP), :]
        slope_row = first_ref[0]
        one, d_one = [], []
        for j in range(GROUP):
            s = smooth[j : j + 1, :]
            kind = kinds[j : j + 1, :]
            term = jnp.where(
                kind == 0.0,
                first_ref[1],
                jnp.where(kind == 1.0, first_ref[2], jnp.where(kind == 2.0, first_ref[3], first_ref[4])),
            )
            x = jnp.tanh(slope_row * s + term)
            d = (1.0 - x * x) * slope_row
            for value, start in ((x, j * 128), (d, half_lanes + j * 128)):
                high, low = split(value)
                in2_ref[0:32, start : start + 128] = high
                in2_ref[32:64, start : start + 128] = low
                in2_ref[64:96, start : start + 128] = high
            one.append(x)
            d_one.append(d)
        pre = dot(weight2, in2_ref[...])
        two, d_two = [], []
        for j in range(GROUP):
            h = jnp.tanh(pre[:, j * 128 : (j + 1) * 128] + bias2_s[...])
            x = h + jnp.concatenate([one[j], one[j]], axis=0)
            d = (1.0 - h * h) * pre[
                :, half_lanes + j * 128 : half_lanes + (j + 1) * 128
            ] + jnp.concatenate([d_one[j], d_one[j]], axis=0)
            for value, start in ((x, j * 128), (d, half_lanes + j * 128)):
                high, low = split(value)
                in3_ref[0:64, start : start + 128] = high
                in3_ref[64:128, start : start + 128] = low
                in3_ref[128:192, start : start + 128] = high
            two.append(x)
            d_two.append(d)
        pre = dot(weight3, in3_ref[...])
        for j in range(GROUP):
            h = jnp.tanh(pre[:, j * 128 : (j + 1) * 128] + bias3_s[...])
            feat_ref[base + j] = h + jnp.concatenate([two[j], two[j]], axis=0)
            tang_ref[base + j] = (1.0 - h * h) * pre[
                :, half_lanes + j * 128 : half_lanes + (j + 1) * 128
            ] + jnp.concatenate([d_two[j], d_two[j]], axis=0)
        envelope = [env_ref[c, pl.ds(base, GROUP), :] for c in range(4)]
        for block in range(16):
            rows = slice(block * 8, block * 8 + 8)
            total = [mom_ref[c, rows, :] for c in range(4)]
            for j in range(GROUP):
                x = feat_ref[base + j, rows, :]
                for c in range(4):
                    total[c] = total[c] + envelope[c][j : j + 1, :] * x
            for c in range(4):
                mom_ref[c, rows, :] = total[c]
        return carry

    lax.fori_loop(0, SLOTS // GROUP, forward, 0)
    mom_ref[...] = mom_ref[...] * (1.0 / SLOTS)

    lead = [mom_ref[c, 0:16, :] for c in range(4)]
    for m in range(100):
        r = m // 25 * 32 + m % 25
        total = mom_ref[0, r : r + 1, :] * lead[0]
        for c in range(1, 4):
            total = total + mom_ref[c, r : r + 1, :] * lead[c]
        desc_ref[m * 16 : m * 16 + 16, :] = total

    fit1_copy.wait()
    weight = split(fit1_ref[...])
    hidden = dot3(weight, split(desc_ref[...]))
    kind = type_ref[...]
    term = jnp.where(
        kind == 0,
        column(9, 0, 240),
        jnp.where(kind == 1, column(10, 0, 240), jnp.where(kind == 2, column(11, 0, 240), column(12, 0, 240))),
    )
    first = jnp.tanh(hidden + term)
    weight_2 = split(fit2_ref[...])
    second = jnp.tanh(dot3(weight_2, split(first)) + column(7, 0, 240))
    lane = lax.broadcasted_iota(jnp.int32, (1, 128), 1)
    own_live = jnp.where(lane < count_ref[0, 0], 1.0, 0.0)
    read = column(8, 0, 240)
    energy = jnp.sum(read * (first + second) * own_live, axis=(0, 1), keepdims=True)
    energy_ref[...] = jnp.broadcast_to(energy, (8, 128))
    upper = read * own_live
    inner = upper * (1.0 - second * second)
    back = upper + dot3(weight_2, split(inner), ((0,), (0,)))
    back = back * (1.0 - first * first)
    flip_ref[...] = jnp.zeros((128, 256), F32)
    flip_ref[:, 0:240] = jnp.transpose(back)
    turned = dot3(split(flip_ref[:, 0:240]), weight)
    for part in range(12):
        desc_ref[part * 128 : (part + 1) * 128, :] = jnp.transpose(turned[:, part * 128 : (part + 1) * 128])
    desc_ref[1536:1600, :] = jnp.transpose(turned[:, 1536:1600])

    grad_mom_ref[...] = jnp.zeros((4, 128, 128), F32)
    gathered = [jnp.zeros((16, 128), F32) for _ in range(4)]
    for m in range(100):
        r = m // 25 * 32 + m % 25
        part = desc_ref[m * 16 : m * 16 + 16, :]
        for c in range(4):
            gathered[c] = gathered[c] + mom_ref[c, r : r + 1, :] * part
            grad_mom_ref[c, r : r + 1, :] = jnp.sum(part * lead[c], axis=0, keepdims=True)
    for c in range(4):
        grad_mom_ref[c, 0:16, :] = grad_mom_ref[c, 0:16, :] + gathered[c]
    grad_mom_ref[...] = grad_mom_ref[...] * (1.0 / SLOTS)

    step = 4

    def backward(group, carry):
        base = pl.multiple_of(group * step, step)
        value = [[jnp.zeros((8, 128), F32) for _ in range(4)] for _ in range(step)]
        slope = [[jnp.zeros((8, 128), F32) for _ in range(4)] for _ in range(step)]
        for block in range(16):
            rows = slice(block * 8, block * 8 + 8)
            grads = [grad_mom_ref[c, rows, :] for c in range(4)]
            for j in range(step):
                x = feat_ref[base + j, rows, :]
                d = tang_ref[base + j, rows, :]
                for c in range(4):
                    value[j][c] = value[j][c] + grads[c] * x
                    slope[j][c] = slope[j][c] + grads[c] * d
        for j in range(step):
            through = jnp.zeros((8, 128), F32)
            for c in range(4):
                through = through + env_ref[c, pl.ds(base + j, 1), :] * slope[j][c]
                den_ref[c, pl.ds(base + j, 1), :] = jnp.sum(value[j][c], axis=0, keepdims=True)
            den_ref[4, pl.ds(base + j, 1), :] = jnp.sum(through, axis=0, keepdims=True)
        return carry

    lax.fori_loop(0, SLOTS // step, backward, 0)

    own = [jnp.zeros((8, 128), F32) for _ in range(3)]
    for group in range(SLOTS // 8):
        rows = slice(group * 8, group * 8 + 8)
        v = [pair_ref[c, rows, :] for c in range(3)]
        inverse = pair_ref[4, rows, :]
        scale = pair_ref[5, rows, :] * inverse * inverse * (1.0 / RANGE)
        by_v = [den_ref[c + 1, rows, :] for c in range(3)]
        along = v[0] * by_v[0] + v[1] * by_v[1] + v[2] * by_v[2]
        radial = inverse * (den_ref[0, rows, :] + den_ref[4, rows, :] + 2.0 * inverse * along)
        for c in range(3):
            grad = scale * (by_v[c] - v[c] * radial)
            pair_ref[c, rows, :] = grad
            own[c] = own[c] - grad
    row8 = lax.broadcasted_iota(jnp.int32, (8, 128), 0)
    own_rows = [jnp.sum(own[c], axis=0, keepdims=True) for c in range(3)]
    own_ref[...] = jnp.where(
        row8[0:4] == 0, own_rows[0], jnp.where(row8[0:4] == 1, own_rows[1], jnp.where(row8[0:4] == 2, own_rows[2], 0.0))
    )

    line = lax.broadcasted_iota(jnp.int32, (48, 128), 0)
    direction = line % 4
    domain = line // 12 + 3 * (line // 4 % 3)
    domain = jnp.where(line < 36, domain, -1)
    atom_index = lax.broadcasted_iota(jnp.int32, (128, 128), 0)

    def scatter(group, total):
        base = pl.multiple_of(group * GROUP, GROUP)
        entry = jnp.maximum(table_ref[pl.ds(base, GROUP), :], 0)
        block = entry // ATOMS
        atom = entry % ATOMS
        grads = [pair_ref[c, pl.ds(base, GROUP), :] for c in range(3)]
        for j in range(GROUP):
            grad = jnp.where(
                direction == 0,
                grads[0][j : j + 1, :],
                jnp.where(direction == 1, grads[1][j : j + 1, :], grads[2][j : j + 1, :]),
            )
            grad = jnp.where((domain == block[j : j + 1, :]) & (direction < 3), grad, 0.0)
            high, low = split(grad)
            left_ref[0:48, j * 128 : (j + 1) * 128] = high
            left_ref[48:96, j * 128 : (j + 1) * 128] = low
            pick_ref[:, j * 128 : (j + 1) * 128] = jnp.where(atom_index == atom[j : j + 1, :], 1.0, 0.0).astype(BF16)
        return total + dot(left_ref[...], pick_ref[...], ((1,), (1,)))

    total = lax.fori_loop(0, SLOTS // GROUP, scatter, jnp.zeros((96, 128), F32))
    total = total[0:48] + total[48:96]
    for col, out in enumerate((out_low, out_mid, out_high)):
        for slab in range(3):
            start = col * 12 + slab * 4
            out[slab] = total[start : start + 4]


def call(kernel, outs, scratch, operands, name, flops, moved, smem=(), left=(), limit=60):
    vmem = pl.BlockSpec(memory_space=pltpu.VMEM)
    scalar = pl.BlockSpec(memory_space=pltpu.SMEM)
    anywhere = pl.BlockSpec(memory_space=pltpu.HBM)
    return pl.pallas_call(
        kernel,
        out_shape=[jax.ShapeDtypeStruct(shape, F32) for shape in outs],
        in_specs=[scalar if i in smem else anywhere if i in left else vmem for i in range(len(operands))],
        out_specs=[vmem] * len(outs),
        scratch_shapes=[pltpu.VMEM(*item) if isinstance(item, tuple) else item for item in scratch],
        name=name,
        cost_estimate=pl.CostEstimate(flops=flops, bytes_accessed=moved, transcendentals=0),
        compiler_params=pltpu.CompilerParams(vmem_limit_bytes=limit * 2**20),
    )(*operands)


def local(
    positions,
    atom_types,
    atom_counts,
    neighbours,
    centroid_owner_atoms,
    centroid_cell_offsets,
    emb_first,
    emb_second,
    emb_second_bias,
    emb_third,
    emb_third_bias,
    fit_first,
    fit_type,
    fit_second,
    fit_second_bias,
    fit_out,
):
    basis_h, basis_l, z_h, z_l, zt_h, zt_l, y_h, y_l, yt_h, yt_l = tables()
    pos = positions.reshape(3, 1, ATOMS)
    kinds = atom_types.reshape(1, ATOMS)
    count = atom_counts.reshape(1, 1)
    owner = centroid_owner_atoms.reshape(1, CENTRES)
    shift = centroid_cell_offsets.reshape(3, 1, CENTRES)
    index = (lax.axis_index("slab") * COLS + lax.axis_index("col")).reshape(1, 1)

    def ring(value, axis, step):
        size = lax.axis_size(axis)
        return lax.ppermute(value, axis, [(i, (i + step) % size) for i in range(size)])

    (packed,) = call(
        pack_kernel,
        [(1, 8, ATOMS)],
        [
            ((8, 256), F32),
            ((3, 1, ATOMS), F32),
            ((1, ATOMS), jnp.int32),
            ((1, CENTRES), jnp.int32),
            ((3, 1, CENTRES), F32),
            pltpu.SemaphoreType.DMA((4,)),
        ],
        [pos, kinds, owner, shift, count],
        "pack",
        1_000_000,
        10_000,
        (4,),
        range(4),
    )
    mid = jnp.concatenate([ring(packed, "slab", 1), packed, ring(packed, "slab", -1)], 0)
    low = ring(mid, "col", 1)
    high = ring(mid, "col", -1)

    (outgoing,) = call(
        spread_kernel,
        [(MESH, 1, CHUNK_IN)],
        [
            ((8, 512), F32),
            ((CELL_Z * PATCH_Y, 512), F32),
            ((CELL_Z * PATCH_Y, 512), F32),
            ((MESH, CHUNK_IN), F32),
        ],
        [mid, basis_h, basis_l],
        "spread",
        5_000_000_000,
        1_000_000,
    )
    outgoing, low, high = lax.optimization_barrier((outgoing, low, high))
    plane = lax.all_to_all(outgoing, BOTH, 0, 0, tiled=True)

    pairs = SLOTS * ATOMS
    short, own, back_mid, back_low, back_high = call(
        short_kernel,
        [(8, 128), (4, 128), (3, 4, 128), (3, 4, 128), (3, 4, 128)],
        [
            ((240, 1600), F32),
            pltpu.SemaphoreType.DMA(()),
            ((256, 128), F32),
            ((128, 256), F32),
            ((6, SLOTS, 128), F32),
            ((4, SLOTS, 128), F32),
            ((5, 32, 128), F32),
            ((128, 128), F32),
            ((256, 128), F32),
            ((64, 128), F32),
            ((128, 128), F32),
            ((96, 2 * GROUP * 128), BF16),
            ((192, 2 * GROUP * 128), BF16),
            ((SLOTS, 128, 128), F32),
            ((SLOTS, 128, 128), F32),
            ((4, 128, 128), F32),
            ((1600, 128), F32),
            ((4, 128, 128), F32),
            ((5, SLOTS, 128), F32),
            ((96, GROUP * 128), BF16),
            ((128, GROUP * 128), BF16),
        ],
        [
            neighbours.reshape(ATOMS, SLOTS).T,
            kinds,
            count,
            mid,
            low,
            high,
            emb_first.T,
            emb_second.T,
            emb_second_bias.reshape(1, -1),
            emb_third.T,
            emb_third_bias.reshape(1, -1),
            fit_first,
            fit_type.T,
            fit_second,
            fit_second_bias.reshape(1, -1),
            fit_out.reshape(1, -1),
        ],
        "short",
        pairs * 400_000,
        4_000_000,
        (2,),
        (11,),
    )

    (returning,) = call(
        solve_kernel,
        [(MESH, 1, CHUNK)],
        [((CHUNK // 128, MESH, 128), F32), ((PATCH_Z * SLABS, PATCH_Y * COLS), F32)],
        [plane, short, index, z_h, z_l, zt_h, zt_l, y_h, y_l, yt_h, yt_l],
        "solve",
        400_000_000,
        2_000_000,
        (2,),
        limit=40,
    )
    potential = lax.all_to_all(returning, BOTH, 0, 0, tiled=True)

    ghosts = back_mid + ring(back_low, "col", -1) + ring(back_high, "col", 1)
    from_low, from_high = ring(ghosts[2], "slab", 1), ring(ghosts[0], "slab", -1)

    energy, atom_force, centre_force = call(
        interpolate_kernel,
        [(1, 128), (3, 1, ATOMS), (3, 1, CENTRES)],
        [((8, 256), F32), ((MESH, CHUNK), F32)],
        [potential, pos, kinds, count, owner, shift, basis_h, basis_l, own, ghosts, from_low, from_high],
        "interpolate",
        600_000_000,
        1_500_000,
        (3,),
        limit=40,
    )
    return energy[0, 0], atom_force.reshape(1, 1, 3, ATOMS), centre_force.reshape(1, 1, 3, CENTRES)


def solution(mesh):
    return jax.shard_map(
        local,
        mesh=mesh,
        in_specs=(
            P("slab", "col", None, None),
            P("slab", "col", None),
            P("slab", "col"),
            P("slab", "col", None, None),
            P("slab", "col", None),
            P("slab", "col", None, None),
            P(),
            P(),
            P(),
            P(),
            P(),
            P(),
            P(),
            P(),
            P(),
            P(),
        ),
        out_specs=(P(), P("slab", "col", None, None), P("slab", "col", None, None)),
        check_vma=False,
    )
```

```python
import functools
import math

import jax
import jax.numpy as jnp
import ml_dtypes
import numpy as np
from jax import lax
from jax.experimental import pallas as pl
from jax.experimental.pallas import tpu as pltpu
from jax.sharding import PartitionSpec as P

CHARGES = (6.0, 1.0, 1.0, -1.0)
WANNIER = -8.0
RANGE = 24.0
COUPLING = 0.05
SMEAR = 0.6
ATOMS = 128
CENTRES = 32
SLOTS = 64
MESH = 256
SLABS, COLS = 32, 8
CELL_Z, CELL_Y = 8, 32
REACH = 3
PATCH_Z, PATCH_Y = 14, 40
PATCH = PATCH_Z * PATCH_Y
CHUNK_IN = 384
CHUNK = 640
GROUP = 16
F32 = jnp.float32
BF16 = jnp.bfloat16
BOTH = ("slab", "col")


def halves(array):
    high = array.astype(ml_dtypes.bfloat16)
    low = (array - high.astype(np.float64)).astype(ml_dtypes.bfloat16)
    return high, low


@functools.lru_cache(maxsize=None)
def tables():
    k = np.arange(MESH)[:, None]
    n = np.arange(MESH)[None, :]
    phase = 2.0 * np.pi * ((k * n) % MESH) / MESH
    basis = np.where(k <= MESH // 2, np.cos(phase), np.sin(phase)) * math.sqrt(2.0 / MESH)
    basis[0] = 1.0 / math.sqrt(MESH)
    basis[MESH // 2] = np.where(np.arange(MESH) % 2 == 0, 1.0, -1.0) / math.sqrt(MESH)
    cells_z = (np.arange(PATCH_Z)[:, None] - REACH + CELL_Z * np.arange(SLABS)[None, :]) % MESH
    along_z = basis[:, cells_z.reshape(-1)]
    cells_z = (np.arange(CELL_Z)[:, None] + CELL_Z * np.arange(SLABS)[None, :]) % MESH
    inside_z = basis[:, cells_z.reshape(-1)]
    cells_y = (np.arange(PATCH_Y)[None, :] - REACH + CELL_Y * np.arange(COLS)[:, None]) % MESH
    along_y = basis[:, cells_y.reshape(-1)].T
    out = []
    for matrix in (basis, inside_z, along_z.T, along_y, along_y.T):
        out.extend(halves(matrix))
    return out


def split(value):
    high = value.astype(BF16)
    return high, (value - high.astype(F32)).astype(BF16)


def dot(left, right, dims=((1,), (0,))):
    return lax.dot_general(left, right, (dims, ((), ())), preferred_element_type=F32)


def dot3(left, right, dims=((1,), (0,))):
    return dot(left[0], right[0], dims) + (dot(left[0], right[1], dims) + dot(left[1], right[0], dims))


def lanes(table, index):
    return jnp.take_along_axis(table, index, axis=1)


def spline(z, slope):
    a = jnp.abs(z)
    a2 = z * z
    rest = 2.5 - a
    rest2 = rest * rest
    inner = 115.0 / 192.0 + a2 * (-0.625 + 0.25 * a2)
    middle = (55.0 + a * (20.0 + a * (-120.0 + a * (80.0 - 16.0 * a)))) * (1.0 / 96.0)
    outer = rest2 * rest2 * (1.0 / 24.0)
    near, mid, far = a < 0.5, a < 1.5, a < 2.5
    value = jnp.where(near, inner, jnp.where(mid, middle, jnp.where(far, outer, 0.0)))
    if not slope:
        return value, None
    d_inner = a * (a2 - 1.25)
    d_middle = (20.0 + a * (-240.0 + a * (240.0 - 64.0 * a))) * (1.0 / 96.0)
    d_outer = rest2 * rest * (-1.0 / 6.0)
    d = jnp.where(near, d_inner, jnp.where(mid, d_middle, jnp.where(far, d_outer, 0.0)))
    return value, jnp.where(z < 0.0, -d, d)


def points(pos_ref, type_ref, count_ref, owner_ref, shift_ref, place_ref):
    lane = lax.broadcasted_iota(jnp.int32, (8, 128), 1)
    place_ref[...] = jnp.zeros((8, 256), F32)
    place_ref[0:3, 0:128] = pos_ref[:, 0, :]
    place_ref[0:3, 128:160] = shift_ref[:, 0, :]
    place_ref[3:4, 128:160] = owner_ref[...].astype(F32)
    row = lax.broadcasted_iota(jnp.int32, (8, 128), 0)
    extent = jnp.where(row == 0, float(MESH), jnp.where(row == 1, float(CELL_Y), float(CELL_Z)))
    atoms = place_ref[:, 0:128] * extent
    owner = jnp.where(lane < CENTRES, place_ref[3:4, 128:256].astype(jnp.int32), -1)
    carrying = jnp.broadcast_to(jnp.maximum(owner, 0), (8, 128))
    centres = lanes(atoms, carrying) + place_ref[:, 128:256]
    kind = type_ref[...]
    charge = jnp.where(
        kind == 0, CHARGES[0], jnp.where(kind == 1, CHARGES[1], jnp.where(kind == 2, CHARGES[2], CHARGES[3]))
    )
    charge = jnp.where(lane[0:1] < count_ref[0, 0], charge, 0.0)
    centre_charge = jnp.where(owner[0:1] >= 0, WANNIER, 0.0)
    place_ref[:, 0:128] = atoms
    place_ref[:, 128:256] = centres
    return jnp.concatenate([charge, centre_charge], axis=1), owner[0:1]


def offsets(coordinate, cells, low):
    cell = lax.broadcasted_iota(jnp.int32, (cells, coordinate.shape[1]), 0) + low
    return coordinate - cell.astype(F32) - 0.5


def wrapped(z):
    return z - float(MESH) * jnp.round(z * (1.0 / MESH))


def pack_kernel(*refs):
    sources, (count_ref, out_ref, place_ref), copies, sems = refs[:4], refs[4:7], refs[7:11], refs[11]
    moves = [pltpu.make_async_copy(a, b, sems.at[i]) for i, (a, b) in enumerate(zip(sources, copies))]
    for move in moves:
        move.start()
    for move in moves:
        move.wait()
    pos_ref, type_ref, owner_ref, shift_ref = copies
    charge, _ = points(pos_ref, type_ref, count_ref, owner_ref, shift_ref, place_ref)
    out_ref[0] = jnp.zeros((8, 128), F32)
    out_ref[0, 0:3, :] = place_ref[0:3, 0:128]
    out_ref[0, 3:4, :] = type_ref[...].astype(F32)
    out_ref[0, 4:5, :] = charge[:, 0:128]
    for c in range(3):
        out_ref[0, 5:6, c * 32 : c * 32 + 32] = place_ref[c : c + 1, 128:160]
    out_ref[0, 5:6, 96:128] = charge[:, 128:160]


def spread_kernel(mid_ref, basis_h, basis_l, out_ref, place_ref, amp_h, amp_l, all_ref):
    place_ref[...] = jnp.zeros((8, 512), F32)
    for d in range(3):
        shift = (0.0, 0.0, float((d - 1) * CELL_Z), 0.0)
        for c, row in enumerate((0, 1, 2, 4)):
            place_ref[c : c + 1, d * 128 : d * 128 + 128] = mid_ref[d, row : row + 1, :] + shift[c]
            place_ref[c : c + 1, 384 + d * 32 : 416 + d * 32] = mid_ref[d, 5:6, c * 32 : c * 32 + 32] + shift[c]
    along_x, _ = spline(wrapped(offsets(place_ref[0:1, :], MESH, 0)), False)
    along_y, _ = spline(offsets(place_ref[1:2, :], PATCH_Y, -REACH), False)
    along_z, _ = spline(offsets(place_ref[2:3, :], CELL_Z, 0), False)
    along_z = along_z * place_ref[3:4, :]
    for cell in range(CELL_Z):
        block = along_z[cell : cell + 1, :] * along_y
        high = block.astype(BF16).astype(F32)
        amp_h[cell * PATCH_Y : (cell + 1) * PATCH_Y, :] = high
        amp_l[cell * PATCH_Y : (cell + 1) * PATCH_Y, :] = block - high
    spectral = split(dot3((basis_h[...], basis_l[...]), split(along_x)))
    all_ref[...] = jnp.zeros((MESH, CHUNK_IN), F32)
    all_ref[:, 0 : CELL_Z * PATCH_Y] = dot3(
        spectral, (amp_h[...].astype(BF16), amp_l[...].astype(BF16)), ((1,), (1,))
    )
    out_ref[:, 0, :] = all_ref[...]


def solve_kernel(
    plane_ref, short_ref, index_ref, z_h, z_l, zt_h, zt_l, y_h, y_l, yt_h, yt_l, out_ref, all_ref, grid_ref
):
    for tile in range(CHUNK_IN // 128):
        all_ref[tile] = plane_ref[:, 0, tile * 128 : (tile + 1) * 128]
    for col in range(COLS):
        rows = jnp.concatenate(
            [all_ref[tile, pl.ds(col, SLABS, stride=COLS), :] for tile in range(CHUNK_IN // 128)], axis=1
        )
        for cell in range(CELL_Z):
            grid_ref[cell * SLABS : (cell + 1) * SLABS, col * PATCH_Y : (col + 1) * PATCH_Y] = rows[
                :, cell * PATCH_Y : (cell + 1) * PATCH_Y
            ]
    by_y = dot3(split(grid_ref[0 : CELL_Z * SLABS, :]), (y_h[...], y_l[...]))
    spectrum = dot3((z_h[...], z_l[...]), split(by_y))
    unit = 2.0 * math.pi / MESH
    index_z = lax.broadcasted_iota(jnp.int32, (MESH, MESH), 0)
    index_y = lax.broadcasted_iota(jnp.int32, (MESH, MESH), 1)
    index_x = jnp.full((MESH, MESH), index_ref[0, 0], jnp.int32)

    def square_of(index):
        wave = jnp.minimum(index, MESH - index).astype(F32) * unit
        return wave * wave

    square = square_of(index_z) + square_of(index_y) + square_of(index_x)
    nonzero = square > 0.0
    safe = jnp.where(nonzero, square, 1.0)
    green = jnp.where(nonzero, 4.0 * math.pi * jnp.exp(-0.5 * SMEAR * SMEAR * square) / safe, 0.0)
    filtered = spectrum * green
    energy = 0.5 * COUPLING * jnp.sum(spectrum * filtered, axis=(0, 1), keepdims=True)
    energy = energy + short_ref[0, 0]
    back_z = dot3((zt_h[...], zt_l[...]), split(filtered))
    grid_ref[...] = dot3(split(back_z), (yt_h[...], yt_l[...]))
    tail = jnp.broadcast_to(energy, (SLABS, CHUNK - PATCH))
    for col in range(COLS):
        pieces = [
            grid_ref[cell * SLABS : (cell + 1) * SLABS, col * PATCH_Y : (col + 1) * PATCH_Y]
            for cell in range(PATCH_Z)
        ]
        rows = jnp.concatenate(pieces + [tail], axis=1)
        for tile in range(CHUNK // 128):
            all_ref[tile, pl.ds(col, SLABS, stride=COLS), :] = rows[:, tile * 128 : (tile + 1) * 128]
    for tile in range(CHUNK // 128):
        out_ref[:, 0, tile * 128 : (tile + 1) * 128] = all_ref[tile]


def weigh_kernel(
    pos_ref,
    type_ref,
    count_ref,
    owner_ref,
    shift_ref,
    basis_h,
    basis_l,
    spectral_h,
    spectral_l,
    along_ref,
    slope_ref,
    point_ref,
    place_ref,
):
    charge, owner = points(pos_ref, type_ref, count_ref, owner_ref, shift_ref, place_ref)
    basis = (basis_h[...], basis_l[...])
    along_x, slope_x = spline(wrapped(offsets(place_ref[0:1, :], MESH, 0)), True)
    for start, weight in ((0, along_x), (256, slope_x)):
        high, low = split(dot3(basis, split(weight)))
        spectral_h[:, start : start + 256] = high
        spectral_l[:, start : start + 256] = low
    along_ref[0:PATCH_Y, :], slope_ref[0:PATCH_Y, :] = spline(offsets(place_ref[1:2, :], PATCH_Y, -REACH), True)
    along_ref[PATCH_Y:56, :], slope_ref[PATCH_Y:56, :] = spline(offsets(place_ref[2:3, :], 16, -REACH), True)
    point_ref[...] = jnp.zeros((8, 256), F32)
    point_ref[0:1, :] = -COUPLING * charge
    point_ref[1:2, 0:128] = owner.astype(F32)


def interpolate_kernel(
    back_ref,
    spectral_h,
    spectral_l,
    along_ref,
    slope_ref,
    point_ref,
    own_ref,
    kept_ref,
    from_low,
    from_high,
    energy_ref,
    atom_ref,
    centre_ref,
    all_ref,
):
    along_y, along_z = along_ref[0:PATCH_Y, :], along_ref[PATCH_Y:56, :]
    slope_y, slope_z = slope_ref[0:PATCH_Y, :], slope_ref[PATCH_Y:56, :]
    owner = point_ref[1:2, 0:128].astype(jnp.int32)
    all_ref[...] = back_ref[:, 0, :]
    energy_ref[...] = jnp.broadcast_to(
        jnp.sum(all_ref[:, PATCH : PATCH + 1], axis=(0, 1), keepdims=True)
        * (1.0 / (ATOMS * SLABS * COLS)),
        (1, 128),
    )
    turned = split(jnp.transpose(all_ref[...])[0:PATCH, :])
    both = dot3(turned, (spectral_h[...], spectral_l[...]))
    values, slopes = both[:, 0:256], both[:, 256:512]
    by_x = jnp.zeros((PATCH_Y, 256), F32)
    by_y = jnp.zeros((PATCH_Y, 256), F32)
    by_z = jnp.zeros((PATCH_Y, 256), F32)
    for cell in range(PATCH_Z):
        part = values[cell * PATCH_Y : (cell + 1) * PATCH_Y, :]
        by_x = by_x + along_z[cell : cell + 1, :] * slopes[cell * PATCH_Y : (cell + 1) * PATCH_Y, :]
        by_y = by_y + along_z[cell : cell + 1, :] * part
        by_z = by_z + slope_z[cell : cell + 1, :] * part
    scale = point_ref[0:1, :]
    force_x = jnp.sum(along_y * by_x, axis=0, keepdims=True) * scale
    force_y = jnp.sum(slope_y * by_y, axis=0, keepdims=True) * scale
    force_z = jnp.sum(along_y * by_z, axis=0, keepdims=True) * scale
    row = lax.broadcasted_iota(jnp.int32, (8, 256), 0)
    force = jnp.where(
        row == 0, force_x, jnp.where(row == 1, force_y, jnp.where(row == 2, force_z, 0.0))
    )
    atom_index = lax.broadcasted_iota(jnp.int32, (128, 128), 0)
    picker = jnp.where(atom_index == owner, 1.0, 0.0).astype(BF16)
    centre = force[:, 128:256]
    high, low = split(centre)
    lower = (centre - high.astype(F32) - low.astype(F32)).astype(BF16)
    dims = ((1,), (1,))
    carried = dot(high, picker, dims) + (dot(low, picker, dims) + dot(lower, picker, dims))
    short = (own_ref[...] + kept_ref[1]) + (from_low[...] + from_high[...])
    atom_ref[:, 0, :] = force[0:3, 0:128] + carried[0:3] - short[0:3]
    centre_ref[:, 0, :] = force[0:3, 128:160]


def short_kernel(
    table_ref,
    type_ref,
    count_ref,
    mid_ref,
    low_ref,
    high_ref,
    emb1_ref,
    emb2_ref,
    bias2_ref,
    emb3_ref,
    bias3_ref,
    fit1_hbm,
    fit_type_ref,
    fit2_ref,
    fit_bias_ref,
    fit_out_ref,
    energy_ref,
    own_ref,
    out_mid,
    out_low,
    out_high,
    fit1_ref,
    fit1_sem,
    turn_ref,
    flip_ref,
    pair_ref,
    env_ref,
    first_ref,
    second_ref,
    third_ref,
    bias2_s,
    bias3_s,
    in2_ref,
    in3_ref,
    feat_ref,
    tang_ref,
    mom_ref,
    desc_ref,
    grad_mom_ref,
    den_ref,
    left_ref,
    pick_ref,
):
    ghost_refs = (low_ref, mid_ref, high_ref)
    fit1_copy = pltpu.make_async_copy(fit1_hbm, fit1_ref, fit1_sem)
    fit1_copy.start()
    centre = [mid_ref[1, c : c + 1, :] for c in range(3)]

    for group in range(SLOTS // 8):
        rows = slice(group * 8, group * 8 + 8)
        entry = table_ref[rows, :]
        live = jnp.where(entry >= 0, 1.0, 0.0)
        entry = jnp.maximum(entry, 0)
        block = entry >> 7
        atom = entry & (ATOMS - 1)
        near = [jnp.zeros((8, 128), F32) for _ in range(4)]
        for b in range(9):
            ghost = ghost_refs[b % 3]
            here = block == b
            for c in range(4):
                line = ghost[b // 3, c : c + 1, :]
                if c == 1:
                    line = line + float((b % 3 - 1) * CELL_Y)
                if c == 2:
                    line = line + float((b // 3 - 1) * CELL_Z)
                near[c] = jnp.where(here, lanes(jnp.broadcast_to(line, (8, 128)), atom), near[c])
        v = [(near[c] - centre[c]) * (1.0 / RANGE) for c in range(3)]
        inverse = 1.0 / jnp.sqrt(1.0 + (v[0] * v[0] + v[1] * v[1] + v[2] * v[2]))
        for c in range(3):
            pair_ref[c, rows, :] = v[c]
            env_ref[c + 1, rows, :] = live * v[c] * inverse * inverse
        pair_ref[3, rows, :] = near[3]
        pair_ref[4, rows, :] = inverse
        pair_ref[5, rows, :] = live
        env_ref[0, rows, :] = live * inverse

    flip_ref[...] = jnp.zeros((128, 256), F32)
    flip_ref[0:5, 0:25] = emb1_ref[...]
    flip_ref[5:6, 0:50] = bias2_ref[...]
    flip_ref[6:7, 0:100] = bias3_ref[...]
    flip_ref[7:8, 0:240] = fit_bias_ref[...]
    flip_ref[8:9, 0:240] = fit_out_ref[...]
    flip_ref[9:13, 0:240] = fit_type_ref[...]
    turn_ref[...] = jnp.transpose(flip_ref[...])

    def column(at, start, stop):
        return jnp.broadcast_to(turn_ref[start:stop, at : at + 1], (stop - start, 128))

    first_ref[...] = jnp.zeros((5, 32, 128), F32)
    for c in range(5):
        first_ref[c, 0:25, :] = column(c, 0, 25)
    bias2_s[...] = jnp.zeros((64, 128), F32)
    for half in range(2):
        bias2_s[half * 32 : half * 32 + 25, :] = column(5, half * 25, half * 25 + 25)
    bias3_s[...] = jnp.zeros((104, 128), F32)
    for quarter in range(4):
        bias3_s[quarter * 24 : quarter * 24 + 24, :] = column(6, quarter * 25, quarter * 25 + 24)
        bias3_s[96 + quarter : 97 + quarter, :] = column(6, quarter * 25 + 24, quarter * 25 + 25)
    second_ref[...] = jnp.zeros((128, 128), F32)
    third_ref[...] = jnp.zeros((256, 128), F32)
    for half in range(2):
        block = emb2_ref[:, half * 25 : half * 25 + 25]
        high = block.astype(BF16).astype(F32)
        for stack, part in enumerate((high, high, block - high)):
            second_ref[stack * 32 : stack * 32 + 25, half * 32 : half * 32 + 25] = part
    for quarter in range(4):
        for half in range(2):
            block = emb3_ref[half * 25 : half * 25 + 25, quarter * 25 : quarter * 25 + 25]
            high = block.astype(BF16).astype(F32)
            for stack, part in enumerate((high, high, block - high)):
                start = stack * 64 + half * 32
                third_ref[start : start + 25, quarter * 24 : quarter * 24 + 24] = part[:, 0:24]
                third_ref[start : start + 25, 96 + quarter : 97 + quarter] = part[:, 24:25]
    weight2 = jnp.transpose(second_ref[...])[0:64, 0:96].astype(BF16)
    weight3 = jnp.transpose(third_ref[...])[0:104, 0:192].astype(BF16)
    mom_ref[...] = jnp.zeros((4, 104, 128), F32)
    half_lanes = GROUP * 128
    row8 = lax.broadcasted_iota(jnp.int32, (8, 128), 0)

    def forward(group, carry):
        base = pl.multiple_of(group * GROUP, GROUP)
        smooth = env_ref[0, pl.ds(base, GROUP), :]
        kinds = pair_ref[3, pl.ds(base, GROUP), :]
        slope_row = first_ref[0]
        one, d_one = [], []
        for j in range(GROUP):
            s = smooth[j : j + 1, :]
            kind = kinds[j : j + 1, :]
            term = jnp.where(
                kind == 0.0,
                first_ref[1],
                jnp.where(kind == 1.0, first_ref[2], jnp.where(kind == 2.0, first_ref[3], first_ref[4])),
            )
            x = jnp.tanh(slope_row * s + term)
            d = (1.0 - x * x) * slope_row
            for value, start in ((x, j * 128), (d, half_lanes + j * 128)):
                high, low = split(value)
                in2_ref[0:32, start : start + 128] = high
                in2_ref[32:64, start : start + 128] = low
                in2_ref[64:96, start : start + 128] = high
            one.append(x)
            d_one.append(d)
        pre = dot(weight2, in2_ref[...])
        two, d_two = [], []
        for j in range(GROUP):
            h = jnp.tanh(pre[:, j * 128 : (j + 1) * 128] + bias2_s[...])
            x = h + jnp.concatenate([one[j], one[j]], axis=0)
            d = (1.0 - h * h) * pre[
                :, half_lanes + j * 128 : half_lanes + (j + 1) * 128
            ] + jnp.concatenate([d_one[j], d_one[j]], axis=0)
            for value, start in ((x, j * 128), (d, half_lanes + j * 128)):
                high, low = split(value)
                in3_ref[0:64, start : start + 128] = high
                in3_ref[64:128, start : start + 128] = low
                in3_ref[128:192, start : start + 128] = high
            two.append(x)
            d_two.append(d)
        pre = dot(weight3, in3_ref[...])

        def folded(value):
            last = jnp.where(row8 < 4, jnp.where(row8 % 2 == 0, value[24:25], value[56:57]), 0.0)
            return jnp.concatenate([value[0:24], value[32:56], value[0:24], value[32:56], last], axis=0)

        for j in range(GROUP):
            h = jnp.tanh(pre[:, j * 128 : (j + 1) * 128] + bias3_s[...])
            feat_ref[base + j] = h + folded(two[j])
            tang_ref[base + j] = (1.0 - h * h) * pre[
                :, half_lanes + j * 128 : half_lanes + (j + 1) * 128
            ] + folded(d_two[j])
        envelope = [env_ref[c, pl.ds(base, GROUP), :] for c in range(4)]
        for block in range(13):
            rows = slice(block * 8, block * 8 + 8)
            total = [mom_ref[c, rows, :] for c in range(4)]
            for j in range(GROUP):
                x = feat_ref[base + j, rows, :]
                for c in range(4):
                    total[c] = total[c] + envelope[c][j : j + 1, :] * x
            for c in range(4):
                mom_ref[c, rows, :] = total[c]
        return carry

    lax.fori_loop(0, SLOTS // GROUP, forward, 0)
    mom_ref[...] = mom_ref[...] * (1.0 / SLOTS)

    lead = [mom_ref[c, 0:16, :] for c in range(4)]
    for m in range(100):
        r = m // 25 * 24 + m % 25 if m % 25 < 24 else 96 + m // 25
        total = mom_ref[0, r : r + 1, :] * lead[0]
        for c in range(1, 4):
            total = total + mom_ref[c, r : r + 1, :] * lead[c]
        desc_ref[m * 16 : m * 16 + 16, :] = total

    fit1_copy.wait()
    weight = split(fit1_ref[...])
    hidden = dot3(weight, split(desc_ref[...]))
    kind = type_ref[...]
    term = jnp.where(
        kind == 0,
        column(9, 0, 240),
        jnp.where(kind == 1, column(10, 0, 240), jnp.where(kind == 2, column(11, 0, 240), column(12, 0, 240))),
    )
    first = jnp.tanh(hidden + term)
    weight_2 = split(fit2_ref[...])
    second = jnp.tanh(dot3(weight_2, split(first)) + column(7, 0, 240))
    lane = lax.broadcasted_iota(jnp.int32, (1, 128), 1)
    own_live = jnp.where(lane < count_ref[0, 0], 1.0, 0.0)
    read = column(8, 0, 240)
    energy = jnp.sum(read * (first + second) * own_live, axis=(0, 1), keepdims=True)
    energy_ref[0, 0] = energy[0, 0]
    upper = read * own_live
    inner = upper * (1.0 - second * second)
    back = upper + dot3(weight_2, split(inner), ((0,), (0,)))
    back = back * (1.0 - first * first)
    flip_ref[...] = jnp.zeros((128, 256), F32)
    flip_ref[:, 0:240] = jnp.transpose(back)
    turned = dot3(split(flip_ref[:, 0:240]), weight)
    for part in range(12):
        desc_ref[part * 128 : (part + 1) * 128, :] = jnp.transpose(turned[:, part * 128 : (part + 1) * 128])
    desc_ref[1536:1600, :] = jnp.transpose(turned[:, 1536:1600])

    grad_mom_ref[...] = jnp.zeros((4, 104, 128), F32)
    gathered = [jnp.zeros((16, 128), F32) for _ in range(4)]
    for m in range(100):
        r = m // 25 * 24 + m % 25 if m % 25 < 24 else 96 + m // 25
        part = desc_ref[m * 16 : m * 16 + 16, :]
        for c in range(4):
            gathered[c] = gathered[c] + mom_ref[c, r : r + 1, :] * part
            grad_mom_ref[c, r : r + 1, :] = jnp.sum(part * lead[c], axis=0, keepdims=True)
    for c in range(4):
        grad_mom_ref[c, 0:16, :] = grad_mom_ref[c, 0:16, :] + gathered[c]
    grad_mom_ref[...] = grad_mom_ref[...] * (1.0 / SLOTS)

    step = 4

    def backward(group, carry):
        base = pl.multiple_of(group * step, step)
        value = [[jnp.zeros((8, 128), F32) for _ in range(4)] for _ in range(step)]
        slope = [[jnp.zeros((8, 128), F32) for _ in range(4)] for _ in range(step)]
        for block in range(13):
            rows = slice(block * 8, block * 8 + 8)
            grads = [grad_mom_ref[c, rows, :] for c in range(4)]
            for j in range(step):
                x = feat_ref[base + j, rows, :]
                d = tang_ref[base + j, rows, :]
                for c in range(4):
                    value[j][c] = value[j][c] + grads[c] * x
                    slope[j][c] = slope[j][c] + grads[c] * d
        for j in range(step):
            through = jnp.zeros((8, 128), F32)
            for c in range(4):
                through = through + env_ref[c, pl.ds(base + j, 1), :] * slope[j][c]
                den_ref[c, pl.ds(base + j, 1), :] = jnp.sum(value[j][c], axis=0, keepdims=True)
            den_ref[4, pl.ds(base + j, 1), :] = jnp.sum(through, axis=0, keepdims=True)
        return carry

    lax.fori_loop(0, SLOTS // step, backward, 0)

    own = [jnp.zeros((8, 128), F32) for _ in range(3)]
    for group in range(SLOTS // 8):
        rows = slice(group * 8, group * 8 + 8)
        v = [pair_ref[c, rows, :] for c in range(3)]
        inverse = pair_ref[4, rows, :]
        scale = pair_ref[5, rows, :] * inverse * inverse * (1.0 / RANGE)
        by_v = [den_ref[c + 1, rows, :] for c in range(3)]
        along = v[0] * by_v[0] + v[1] * by_v[1] + v[2] * by_v[2]
        radial = inverse * (den_ref[0, rows, :] + den_ref[4, rows, :] + 2.0 * inverse * along)
        for c in range(3):
            grad = scale * (by_v[c] - v[c] * radial)
            pair_ref[c, rows, :] = grad
            own[c] = own[c] - grad
    own_rows = [jnp.sum(own[c], axis=0, keepdims=True) for c in range(3)]
    own_ref[...] = jnp.where(
        row8[0:4] == 0, own_rows[0], jnp.where(row8[0:4] == 1, own_rows[1], jnp.where(row8[0:4] == 2, own_rows[2], 0.0))
    )

    line = lax.broadcasted_iota(jnp.int32, (48, 128), 0)
    direction = line % 4
    domain = line // 12 + 3 * (line // 4 % 3)
    domain = jnp.where(line < 36, domain, -1)
    atom_index = lax.broadcasted_iota(jnp.int32, (128, 128), 0)

    def scatter(group, total):
        base = pl.multiple_of(group * GROUP, GROUP)
        entry = jnp.maximum(table_ref[pl.ds(base, GROUP), :], 0)
        block = entry >> 7
        atom = entry & (ATOMS - 1)
        grads = [pair_ref[c, pl.ds(base, GROUP), :] for c in range(3)]
        for j in range(GROUP):
            grad = jnp.where(
                direction == 0,
                grads[0][j : j + 1, :],
                jnp.where(direction == 1, grads[1][j : j + 1, :], grads[2][j : j + 1, :]),
            )
            grad = jnp.where((domain == block[j : j + 1, :]) & (direction < 3), grad, 0.0)
            high, low = split(grad)
            left_ref[0:48, j * 128 : (j + 1) * 128] = high
            left_ref[48:96, j * 128 : (j + 1) * 128] = low
            pick_ref[:, j * 128 : (j + 1) * 128] = jnp.where(atom_index == atom[j : j + 1, :], 1.0, 0.0).astype(BF16)
        return total + dot(left_ref[...], pick_ref[...], ((1,), (1,)))

    total = lax.fori_loop(0, SLOTS // GROUP, scatter, jnp.zeros((96, 128), F32))
    total = total[0:48] + total[48:96]
    for col, out in enumerate((out_low, out_mid, out_high)):
        for slab in range(3):
            start = col * 12 + slab * 4
            out[slab] = total[start : start + 4]


def call(kernel, outs, scratch, operands, name, flops, moved, smem=(), left=(), limit=60):
    vmem = pl.BlockSpec(memory_space=pltpu.VMEM)
    scalar = pl.BlockSpec(memory_space=pltpu.SMEM)
    anywhere = pl.BlockSpec(memory_space=pltpu.HBM)
    return pl.pallas_call(
        kernel,
        out_shape=[
            jax.ShapeDtypeStruct(*item) if isinstance(item[0], tuple) else jax.ShapeDtypeStruct(item, F32) for item in outs
        ],
        in_specs=[scalar if i in smem else anywhere if i in left else vmem for i in range(len(operands))],
        out_specs=[scalar if shape == (1, 1) else vmem for shape in outs],
        scratch_shapes=[pltpu.VMEM(*item) if isinstance(item, tuple) else item for item in scratch],
        name=name,
        cost_estimate=pl.CostEstimate(flops=flops, bytes_accessed=moved, transcendentals=0),
        compiler_params=pltpu.CompilerParams(vmem_limit_bytes=limit * 2**20),
    )(*operands)


def local(
    positions,
    atom_types,
    atom_counts,
    neighbours,
    centroid_owner_atoms,
    centroid_cell_offsets,
    emb_first,
    emb_second,
    emb_second_bias,
    emb_third,
    emb_third_bias,
    fit_first,
    fit_type,
    fit_second,
    fit_second_bias,
    fit_out,
):
    basis_h, basis_l, z_h, z_l, zt_h, zt_l, y_h, y_l, yt_h, yt_l = tables()
    pos = positions.reshape(3, 1, ATOMS)
    kinds = atom_types.reshape(1, ATOMS)
    count = atom_counts.reshape(1, 1)
    owner = centroid_owner_atoms.reshape(1, CENTRES)
    shift = centroid_cell_offsets.reshape(3, 1, CENTRES)
    index = (lax.axis_index("slab") * COLS + lax.axis_index("col")).reshape(1, 1)

    def ring(value, axis, step):
        size = lax.axis_size(axis)
        return lax.ppermute(value, axis, [(i, (i + step) % size) for i in range(size)])

    (packed,) = call(
        pack_kernel,
        [(1, 8, ATOMS)],
        [
            ((8, 256), F32),
            ((3, 1, ATOMS), F32),
            ((1, ATOMS), jnp.int32),
            ((1, CENTRES), jnp.int32),
            ((3, 1, CENTRES), F32),
            pltpu.SemaphoreType.DMA((4,)),
        ],
        [pos, kinds, owner, shift, count],
        "pack",
        1_000_000,
        10_000,
        (4,),
        range(4),
    )
    mid = jnp.concatenate([ring(packed, "slab", 1), packed, ring(packed, "slab", -1)], 0)
    low = ring(mid, "col", 1)
    high = ring(mid, "col", -1)

    (outgoing,) = call(
        spread_kernel,
        [(MESH, 1, CHUNK_IN)],
        [
            ((8, 512), F32),
            ((CELL_Z * PATCH_Y, 512), F32),
            ((CELL_Z * PATCH_Y, 512), F32),
            ((MESH, CHUNK_IN), F32),
        ],
        [mid, basis_h, basis_l],
        "spread",
        5_000_000_000,
        1_000_000,
    )
    outgoing, low, high = lax.optimization_barrier((outgoing, low, high))
    plane = lax.all_to_all(outgoing, BOTH, 0, 0, tiled=True)

    pairs = SLOTS * ATOMS
    short, own, back_mid, back_low, back_high = call(
        short_kernel,
        [(1, 1), (4, 128), (3, 4, 128), (3, 4, 128), (3, 4, 128)],
        [
            ((240, 1600), F32),
            pltpu.SemaphoreType.DMA(()),
            ((256, 128), F32),
            ((128, 256), F32),
            ((6, SLOTS, 128), F32),
            ((4, SLOTS, 128), F32),
            ((5, 32, 128), F32),
            ((128, 128), F32),
            ((256, 128), F32),
            ((64, 128), F32),
            ((104, 128), F32),
            ((96, 2 * GROUP * 128), BF16),
            ((192, 2 * GROUP * 128), BF16),
            ((SLOTS, 104, 128), F32),
            ((SLOTS, 104, 128), F32),
            ((4, 104, 128), F32),
            ((1600, 128), F32),
            ((4, 104, 128), F32),
            ((5, SLOTS, 128), F32),
            ((96, GROUP * 128), BF16),
            ((128, GROUP * 128), BF16),
        ],
        [
            neighbours.reshape(ATOMS, SLOTS).T,
            kinds,
            count,
            mid,
            low,
            high,
            emb_first.T,
            emb_second.T,
            emb_second_bias.reshape(1, -1),
            emb_third.T,
            emb_third_bias.reshape(1, -1),
            fit_first,
            fit_type.T,
            fit_second,
            fit_second_bias.reshape(1, -1),
            fit_out.reshape(1, -1),
        ],
        "short",
        pairs * 400_000,
        4_000_000,
        (2,),
        (11,),
    )

    (returning,) = call(
        solve_kernel,
        [(MESH, 1, CHUNK)],
        [((CHUNK // 128, MESH, 128), F32), ((PATCH_Z * SLABS, PATCH_Y * COLS), F32)],
        [plane, short, index, z_h, z_l, zt_h, zt_l, y_h, y_l, yt_h, yt_l],
        "solve",
        400_000_000,
        2_000_000,
        (1, 2),
        limit=40,
    )
    potential = lax.all_to_all(returning, BOTH, 0, 0, tiled=True)

    ghosts = back_mid + ring(back_low, "col", -1) + ring(back_high, "col", 1)
    ghosts, pos = lax.optimization_barrier((ghosts, pos))
    weights = call(
        weigh_kernel,
        [((MESH, 512), BF16), ((MESH, 512), BF16), (56, 256), (56, 256), (8, 256)],
        [((8, 256), F32)],
        [pos, kinds, count, owner, shift, basis_h, basis_l],
        "weigh",
        400_000_000,
        1_000_000,
        (2,),
        limit=40,
    )
    from_low, from_high = ring(ghosts[2], "slab", 1), ring(ghosts[0], "slab", -1)

    energy, atom_force, centre_force = call(
        interpolate_kernel,
        [(1, 128), (3, 1, ATOMS), (3, 1, CENTRES)],
        [((MESH, CHUNK), F32)],
        [potential, *weights, own, ghosts, from_low, from_high],
        "interpolate",
        600_000_000,
        1_500_000,
        limit=40,
    )
    return energy[0, 0], atom_force.reshape(1, 1, 3, ATOMS), centre_force.reshape(1, 1, 3, CENTRES)


def solution(mesh):
    return jax.shard_map(
        local,
        mesh=mesh,
        in_specs=(
            P("slab", "col", None, None),
            P("slab", "col", None),
            P("slab", "col"),
            P("slab", "col", None, None),
            P("slab", "col", None),
            P("slab", "col", None, None),
            P(),
            P(),
            P(),
            P(),
            P(),
            P(),
            P(),
            P(),
            P(),
            P(),
        ),
        out_specs=(P(), P("slab", "col", None, None), P("slab", "col", None, None)),
        check_vma=False,
    )
```

```python
import functools
import math

import jax
import jax.numpy as jnp
import ml_dtypes
import numpy as np
from jax import lax
from jax.experimental import pallas as pl
from jax.experimental.pallas import tpu as pltpu
from jax.sharding import PartitionSpec as P

CHARGES = (6.0, 1.0, 1.0, -1.0)
WANNIER = -8.0
RANGE = 24.0
COUPLING = 0.05
SMEAR = 0.6
ATOMS = 128
CENTRES = 32
SLOTS = 64
MESH = 256
SLABS, COLS = 32, 8
CELL_Z, CELL_Y = 8, 32
REACH = 3
PATCH_Z, PATCH_Y = 14, 40
PATCH = PATCH_Z * PATCH_Y
CHUNK_IN = 384
CHUNK = 640
GROUP = 16
F32 = jnp.float32
BF16 = jnp.bfloat16
BOTH = ("slab", "col")


def halves(array):
    high = array.astype(ml_dtypes.bfloat16)
    low = (array - high.astype(np.float64)).astype(ml_dtypes.bfloat16)
    return high, low


@functools.lru_cache(maxsize=None)
def tables():
    k = np.arange(MESH)[:, None]
    n = np.arange(MESH)[None, :]
    phase = 2.0 * np.pi * ((k * n) % MESH) / MESH
    basis = np.where(k <= MESH // 2, np.cos(phase), np.sin(phase)) * math.sqrt(2.0 / MESH)
    basis[0] = 1.0 / math.sqrt(MESH)
    basis[MESH // 2] = np.where(np.arange(MESH) % 2 == 0, 1.0, -1.0) / math.sqrt(MESH)
    cells_z = (np.arange(PATCH_Z)[:, None] - REACH + CELL_Z * np.arange(SLABS)[None, :]) % MESH
    along_z = basis[:, cells_z.reshape(-1)]
    cells_z = (np.arange(CELL_Z)[:, None] + CELL_Z * np.arange(SLABS)[None, :]) % MESH
    inside_z = basis[:, cells_z.reshape(-1)]
    cells_y = (np.arange(PATCH_Y)[None, :] - REACH + CELL_Y * np.arange(COLS)[:, None]) % MESH
    along_y = basis[:, cells_y.reshape(-1)].T
    out = []
    for matrix in (basis, inside_z, along_z.T, along_y, along_y.T):
        out.extend(halves(matrix))
    return out


def split(value):
    high = value.astype(BF16)
    return high, (value - high.astype(F32)).astype(BF16)


def dot(left, right, dims=((1,), (0,))):
    return lax.dot_general(left, right, (dims, ((), ())), preferred_element_type=F32)


def dot3(left, right, dims=((1,), (0,))):
    if dims != ((1,), (0,)) or left[0].shape[0] % 16:
        return dot(left[0], right[0], dims) + (dot(left[0], right[1], dims) + dot(left[1], right[0], dims))
    rows = left[0].shape[0]
    both = dot(jnp.concatenate(left, axis=0), right[0])
    return both[0:rows] + (both[rows:] + dot(left[0], right[1]))


def lanes(table, index):
    return jnp.take_along_axis(table, index, axis=1)


def spline(z, slope):
    a = jnp.abs(z)
    a2 = z * z
    rest = 2.5 - a
    rest2 = rest * rest
    inner = 115.0 / 192.0 + a2 * (-0.625 + 0.25 * a2)
    middle = (55.0 + a * (20.0 + a * (-120.0 + a * (80.0 - 16.0 * a)))) * (1.0 / 96.0)
    outer = rest2 * rest2 * (1.0 / 24.0)
    near, mid, far = a < 0.5, a < 1.5, a < 2.5
    value = jnp.where(near, inner, jnp.where(mid, middle, jnp.where(far, outer, 0.0)))
    if not slope:
        return value, None
    d_inner = a * (a2 - 1.25)
    d_middle = (20.0 + a * (-240.0 + a * (240.0 - 64.0 * a))) * (1.0 / 96.0)
    d_outer = rest2 * rest * (-1.0 / 6.0)
    d = jnp.where(near, d_inner, jnp.where(mid, d_middle, jnp.where(far, d_outer, 0.0)))
    return value, jnp.where(z < 0.0, -d, d)


def points(pos_ref, type_ref, count_ref, owner_ref, shift_ref, place_ref):
    lane = lax.broadcasted_iota(jnp.int32, (8, 128), 1)
    place_ref[...] = jnp.zeros((8, 256), F32)
    place_ref[0:3, 0:128] = pos_ref[:, 0, :]
    place_ref[0:3, 128:160] = shift_ref[:, 0, :]
    place_ref[3:4, 128:160] = owner_ref[...].astype(F32)
    row = lax.broadcasted_iota(jnp.int32, (8, 128), 0)
    extent = jnp.where(row == 0, float(MESH), jnp.where(row == 1, float(CELL_Y), float(CELL_Z)))
    atoms = place_ref[:, 0:128] * extent
    owner = jnp.where(lane < CENTRES, place_ref[3:4, 128:256].astype(jnp.int32), -1)
    carrying = jnp.broadcast_to(jnp.maximum(owner, 0), (8, 128))
    centres = lanes(atoms, carrying) + place_ref[:, 128:256]
    kind = type_ref[...]
    charge = jnp.where(
        kind == 0, CHARGES[0], jnp.where(kind == 1, CHARGES[1], jnp.where(kind == 2, CHARGES[2], CHARGES[3]))
    )
    charge = jnp.where(lane[0:1] < count_ref[0, 0], charge, 0.0)
    centre_charge = jnp.where(owner[0:1] >= 0, WANNIER, 0.0)
    place_ref[:, 0:128] = atoms
    place_ref[:, 128:256] = centres
    return jnp.concatenate([charge, centre_charge], axis=1), owner[0:1]


def offsets(coordinate, cells, low):
    cell = lax.broadcasted_iota(jnp.int32, (cells, coordinate.shape[1]), 0) + low
    return coordinate - cell.astype(F32) - 0.5


def wrapped(z):
    return z - float(MESH) * jnp.round(z * (1.0 / MESH))


def pack_kernel(*refs):
    sources, (count_ref, out_ref, place_ref), copies, sems = refs[:4], refs[4:7], refs[7:11], refs[11]
    moves = [pltpu.make_async_copy(a, b, sems.at[i]) for i, (a, b) in enumerate(zip(sources, copies))]
    for move in moves:
        move.start()
    for move in moves:
        move.wait()
    pos_ref, type_ref, owner_ref, shift_ref = copies
    charge, _ = points(pos_ref, type_ref, count_ref, owner_ref, shift_ref, place_ref)
    out_ref[0] = jnp.zeros((8, 128), F32)
    out_ref[0, 0:3, :] = place_ref[0:3, 0:128]
    out_ref[0, 3:4, :] = type_ref[...].astype(F32)
    out_ref[0, 4:5, :] = charge[:, 0:128]
    for c in range(3):
        out_ref[0, 5:6, c * 32 : c * 32 + 32] = place_ref[c : c + 1, 128:160]
    out_ref[0, 5:6, 96:128] = charge[:, 128:160]


def spread_kernel(mid_ref, basis_h, basis_l, out_ref, place_ref, amp_h, amp_l, all_ref):
    place_ref[...] = jnp.zeros((8, 512), F32)
    for d in range(3):
        shift = (0.0, 0.0, float((d - 1) * CELL_Z), 0.0)
        for c, row in enumerate((0, 1, 2, 4)):
            place_ref[c : c + 1, d * 128 : d * 128 + 128] = mid_ref[d, row : row + 1, :] + shift[c]
            place_ref[c : c + 1, 384 + d * 32 : 416 + d * 32] = mid_ref[d, 5:6, c * 32 : c * 32 + 32] + shift[c]
    along_x, _ = spline(wrapped(offsets(place_ref[0:1, :], MESH, 0)), False)
    along_y, _ = spline(offsets(place_ref[1:2, :], PATCH_Y, -REACH), False)
    along_z, _ = spline(offsets(place_ref[2:3, :], CELL_Z, 0), False)
    along_z = along_z * place_ref[3:4, :]
    for cell in range(CELL_Z):
        block = along_z[cell : cell + 1, :] * along_y
        high = block.astype(BF16).astype(F32)
        amp_h[cell * PATCH_Y : (cell + 1) * PATCH_Y, :] = high
        amp_l[cell * PATCH_Y : (cell + 1) * PATCH_Y, :] = block - high
    spectral = split(dot3((basis_h[...], basis_l[...]), split(along_x)))
    all_ref[...] = jnp.zeros((MESH, CHUNK_IN), F32)
    all_ref[:, 0 : CELL_Z * PATCH_Y] = dot3(
        spectral, (amp_h[...].astype(BF16), amp_l[...].astype(BF16)), ((1,), (1,))
    )
    out_ref[:, 0, :] = all_ref[...]


def solve_kernel(
    plane_ref, short_ref, index_ref, z_h, z_l, zt_h, zt_l, y_h, y_l, yt_h, yt_l, out_ref, all_ref, grid_ref
):
    for tile in range(CHUNK_IN // 128):
        all_ref[tile] = plane_ref[:, 0, tile * 128 : (tile + 1) * 128]
    for col in range(COLS):
        rows = jnp.concatenate(
            [all_ref[tile, pl.ds(col, SLABS, stride=COLS), :] for tile in range(CHUNK_IN // 128)], axis=1
        )
        for cell in range(CELL_Z):
            grid_ref[cell * SLABS : (cell + 1) * SLABS, col * PATCH_Y : (col + 1) * PATCH_Y] = rows[
                :, cell * PATCH_Y : (cell + 1) * PATCH_Y
            ]
    by_y = dot3(split(grid_ref[0 : CELL_Z * SLABS, :]), (y_h[...], y_l[...]))
    spectrum = dot3((z_h[...], z_l[...]), split(by_y))
    unit = 2.0 * math.pi / MESH
    index_z = lax.broadcasted_iota(jnp.int32, (MESH, MESH), 0)
    index_y = lax.broadcasted_iota(jnp.int32, (MESH, MESH), 1)
    index_x = jnp.full((MESH, MESH), index_ref[0, 0], jnp.int32)

    def square_of(index):
        wave = jnp.minimum(index, MESH - index).astype(F32) * unit
        return wave * wave

    square = square_of(index_z) + square_of(index_y) + square_of(index_x)
    nonzero = square > 0.0
    safe = jnp.where(nonzero, square, 1.0)
    green = jnp.where(nonzero, 4.0 * math.pi * jnp.exp(-0.5 * SMEAR * SMEAR * square) / safe, 0.0)
    filtered = spectrum * green
    energy = 0.5 * COUPLING * jnp.sum(spectrum * filtered, axis=(0, 1), keepdims=True)
    energy = energy + short_ref[0, 0]
    back_z = dot3((zt_h[...], zt_l[...]), split(filtered))
    grid_ref[...] = dot3(split(back_z), (yt_h[...], yt_l[...]))
    tail = jnp.broadcast_to(energy, (SLABS, CHUNK - PATCH))
    for col in range(COLS):
        pieces = [
            grid_ref[cell * SLABS : (cell + 1) * SLABS, col * PATCH_Y : (col + 1) * PATCH_Y]
            for cell in range(PATCH_Z)
        ]
        rows = jnp.concatenate(pieces + [tail], axis=1)
        for tile in range(CHUNK // 128):
            all_ref[tile, pl.ds(col, SLABS, stride=COLS), :] = rows[:, tile * 128 : (tile + 1) * 128]
    for tile in range(CHUNK // 128):
        out_ref[:, 0, tile * 128 : (tile + 1) * 128] = all_ref[tile]


def weigh_kernel(
    pos_ref,
    type_ref,
    count_ref,
    owner_ref,
    shift_ref,
    basis_h,
    basis_l,
    spectral_h,
    spectral_l,
    along_ref,
    slope_ref,
    point_ref,
    place_ref,
):
    charge, owner = points(pos_ref, type_ref, count_ref, owner_ref, shift_ref, place_ref)
    basis = (basis_h[...], basis_l[...])
    along_x, slope_x = spline(wrapped(offsets(place_ref[0:1, :], MESH, 0)), True)
    for start, weight in ((0, along_x), (256, slope_x)):
        high, low = split(dot3(basis, split(weight)))
        spectral_h[:, start : start + 256] = high
        spectral_l[:, start : start + 256] = low
    along_ref[0:PATCH_Y, :], slope_ref[0:PATCH_Y, :] = spline(offsets(place_ref[1:2, :], PATCH_Y, -REACH), True)
    along_ref[PATCH_Y:56, :], slope_ref[PATCH_Y:56, :] = spline(offsets(place_ref[2:3, :], 16, -REACH), True)
    point_ref[...] = jnp.zeros((8, 256), F32)
    point_ref[0:1, :] = -COUPLING * charge
    point_ref[1:2, 0:128] = owner.astype(F32)


def interpolate_kernel(
    back_ref,
    spectral_h,
    spectral_l,
    along_ref,
    slope_ref,
    point_ref,
    own_ref,
    kept_ref,
    from_low,
    from_high,
    energy_ref,
    atom_ref,
    centre_ref,
    all_ref,
):
    along_y, along_z = along_ref[0:PATCH_Y, :], along_ref[PATCH_Y:56, :]
    slope_y, slope_z = slope_ref[0:PATCH_Y, :], slope_ref[PATCH_Y:56, :]
    owner = point_ref[1:2, 0:128].astype(jnp.int32)
    all_ref[...] = back_ref[:, 0, :]
    energy_ref[...] = jnp.broadcast_to(
        jnp.sum(all_ref[:, PATCH : PATCH + 1], axis=(0, 1), keepdims=True)
        * (1.0 / (ATOMS * SLABS * COLS)),
        (1, 128),
    )
    turned = split(jnp.transpose(all_ref[...])[0:PATCH, :])
    both = dot3(turned, (spectral_h[...], spectral_l[...]))
    values, slopes = both[:, 0:256], both[:, 256:512]
    by_x = jnp.zeros((PATCH_Y, 256), F32)
    by_y = jnp.zeros((PATCH_Y, 256), F32)
    by_z = jnp.zeros((PATCH_Y, 256), F32)
    for cell in range(PATCH_Z):
        part = values[cell * PATCH_Y : (cell + 1) * PATCH_Y, :]
        by_x = by_x + along_z[cell : cell + 1, :] * slopes[cell * PATCH_Y : (cell + 1) * PATCH_Y, :]
        by_y = by_y + along_z[cell : cell + 1, :] * part
        by_z = by_z + slope_z[cell : cell + 1, :] * part
    scale = point_ref[0:1, :]
    force_x = jnp.sum(along_y * by_x, axis=0, keepdims=True) * scale
    force_y = jnp.sum(slope_y * by_y, axis=0, keepdims=True) * scale
    force_z = jnp.sum(along_y * by_z, axis=0, keepdims=True) * scale
    row = lax.broadcasted_iota(jnp.int32, (8, 256), 0)
    force = jnp.where(
        row == 0, force_x, jnp.where(row == 1, force_y, jnp.where(row == 2, force_z, 0.0))
    )
    atom_index = lax.broadcasted_iota(jnp.int32, (128, 128), 0)
    picker = jnp.where(atom_index == owner, 1.0, 0.0).astype(BF16)
    centre = force[:, 128:256]
    high, low = split(centre)
    lower = (centre - high.astype(F32) - low.astype(F32)).astype(BF16)
    dims = ((1,), (1,))
    carried = dot(high, picker, dims) + (dot(low, picker, dims) + dot(lower, picker, dims))
    short = (own_ref[...] + kept_ref[1]) + (from_low[...] + from_high[...])
    atom_ref[:, 0, :] = force[0:3, 0:128] + carried[0:3] - short[0:3]
    centre_ref[:, 0, :] = force[0:3, 128:160]


def short_kernel(
    table_ref,
    type_ref,
    count_ref,
    mid_ref,
    low_ref,
    high_ref,
    emb1_ref,
    emb2_ref,
    bias2_ref,
    emb3_ref,
    bias3_ref,
    fit1_hbm,
    fit_type_ref,
    fit2_ref,
    fit_bias_ref,
    fit_out_ref,
    energy_ref,
    own_ref,
    out_mid,
    out_low,
    out_high,
    fit1_ref,
    fit1_sem,
    turn_ref,
    flip_ref,
    pair_ref,
    env_ref,
    first_ref,
    second_ref,
    third_ref,
    bias2_s,
    bias3_s,
    in2_ref,
    in3_ref,
    feat_ref,
    tang_ref,
    mom_ref,
    desc_ref,
    grad_mom_ref,
    den_ref,
    left_ref,
    pick_ref,
):
    ghost_refs = (low_ref, mid_ref, high_ref)
    fit1_copy = pltpu.make_async_copy(fit1_hbm, fit1_ref, fit1_sem)
    fit1_copy.start()
    centre = [mid_ref[1, c : c + 1, :] for c in range(3)]

    for group in range(SLOTS // 8):
        rows = slice(group * 8, group * 8 + 8)
        entry = table_ref[rows, :]
        live = jnp.where(entry >= 0, 1.0, 0.0)
        entry = jnp.maximum(entry, 0)
        block = entry >> 7
        atom = entry & (ATOMS - 1)
        near = [jnp.zeros((8, 128), F32) for _ in range(4)]
        for b in range(9):
            ghost = ghost_refs[b % 3]
            here = block == b
            for c in range(4):
                line = ghost[b // 3, c : c + 1, :]
                if c == 1:
                    line = line + float((b % 3 - 1) * CELL_Y)
                if c == 2:
                    line = line + float((b // 3 - 1) * CELL_Z)
                near[c] = jnp.where(here, lanes(jnp.broadcast_to(line, (8, 128)), atom), near[c])
        v = [(near[c] - centre[c]) * (1.0 / RANGE) for c in range(3)]
        inverse = 1.0 / jnp.sqrt(1.0 + (v[0] * v[0] + v[1] * v[1] + v[2] * v[2]))
        for c in range(3):
            pair_ref[c, rows, :] = v[c]
            env_ref[c + 1, rows, :] = live * v[c] * inverse * inverse
        pair_ref[3, rows, :] = near[3]
        pair_ref[4, rows, :] = inverse
        pair_ref[5, rows, :] = live
        env_ref[0, rows, :] = live * inverse

    flip_ref[...] = jnp.zeros((128, 256), F32)
    flip_ref[0:5, 0:25] = emb1_ref[...]
    flip_ref[5:6, 0:50] = bias2_ref[...]
    flip_ref[6:7, 0:100] = bias3_ref[...]
    flip_ref[7:8, 0:240] = fit_bias_ref[...]
    flip_ref[8:9, 0:240] = fit_out_ref[...]
    flip_ref[9:13, 0:240] = fit_type_ref[...]
    turn_ref[...] = jnp.transpose(flip_ref[...])

    def column(at, start, stop):
        return jnp.broadcast_to(turn_ref[start:stop, at : at + 1], (stop - start, 128))

    first_ref[...] = jnp.zeros((5, 32, 128), F32)
    for c in range(5):
        first_ref[c, 0:25, :] = column(c, 0, 25)
    bias2_s[...] = jnp.zeros((64, 128), F32)
    for half in range(2):
        bias2_s[half * 32 : half * 32 + 25, :] = column(5, half * 25, half * 25 + 25)
    bias3_s[...] = jnp.zeros((104, 128), F32)
    for quarter in range(4):
        bias3_s[quarter * 24 : quarter * 24 + 24, :] = column(6, quarter * 25, quarter * 25 + 24)
        bias3_s[96 + quarter : 97 + quarter, :] = column(6, quarter * 25 + 24, quarter * 25 + 25)
    second_ref[...] = jnp.zeros((128, 128), F32)
    third_ref[...] = jnp.zeros((256, 128), F32)
    for half in range(2):
        block = emb2_ref[:, half * 25 : half * 25 + 25]
        high = block.astype(BF16).astype(F32)
        for stack, part in enumerate((high, high, block - high)):
            second_ref[stack * 32 : stack * 32 + 25, half * 32 : half * 32 + 25] = part
    for quarter in range(4):
        for half in range(2):
            block = emb3_ref[half * 25 : half * 25 + 25, quarter * 25 : quarter * 25 + 25]
            high = block.astype(BF16).astype(F32)
            for stack, part in enumerate((high, high, block - high)):
                start = stack * 64 + half * 32
                third_ref[start : start + 25, quarter * 24 : quarter * 24 + 24] = part[:, 0:24]
                third_ref[start : start + 25, 96 + quarter : 97 + quarter] = part[:, 24:25]
    weight2 = jnp.transpose(second_ref[...])[0:64, 0:96].astype(BF16)
    weight3 = jnp.transpose(third_ref[...])[0:104, 0:192].astype(BF16)
    mom_ref[...] = jnp.zeros((4, 104, 128), F32)
    half_lanes = GROUP * 128
    row8 = lax.broadcasted_iota(jnp.int32, (8, 128), 0)

    def forward(group, carry):
        base = pl.multiple_of(group * GROUP, GROUP)
        smooth = env_ref[0, pl.ds(base, GROUP), :]
        kinds = pair_ref[3, pl.ds(base, GROUP), :]
        slope_row = first_ref[0]
        one, d_one = [], []
        for j in range(GROUP):
            s = smooth[j : j + 1, :]
            kind = kinds[j : j + 1, :]
            term = jnp.where(
                kind == 0.0,
                first_ref[1],
                jnp.where(kind == 1.0, first_ref[2], jnp.where(kind == 2.0, first_ref[3], first_ref[4])),
            )
            x = jnp.tanh(slope_row * s + term)
            d = (1.0 - x * x) * slope_row
            for value, start in ((x, j * 128), (d, half_lanes + j * 128)):
                high, low = split(value)
                in2_ref[0:32, start : start + 128] = high
                in2_ref[32:64, start : start + 128] = low
                in2_ref[64:96, start : start + 128] = high
            one.append(x)
            d_one.append(d)
        pre = dot(weight2, in2_ref[...])
        two, d_two = [], []
        for j in range(GROUP):
            h = jnp.tanh(pre[:, j * 128 : (j + 1) * 128] + bias2_s[...])
            x = h + jnp.concatenate([one[j], one[j]], axis=0)
            d = (1.0 - h * h) * pre[
                :, half_lanes + j * 128 : half_lanes + (j + 1) * 128
            ] + jnp.concatenate([d_one[j], d_one[j]], axis=0)
            for value, start in ((x, j * 128), (d, half_lanes + j * 128)):
                high, low = split(value)
                in3_ref[0:64, start : start + 128] = high
                in3_ref[64:128, start : start + 128] = low
                in3_ref[128:192, start : start + 128] = high
            two.append(x)
            d_two.append(d)
        pre = dot(weight3, in3_ref[...])

        def folded(value):
            last = jnp.where(row8 < 4, jnp.where(row8 % 2 == 0, value[24:25], value[56:57]), 0.0)
            return jnp.concatenate([value[0:24], value[32:56], value[0:24], value[32:56], last], axis=0)

        for j in range(GROUP):
            h = jnp.tanh(pre[:, j * 128 : (j + 1) * 128] + bias3_s[...])
            feat_ref[base + j] = h + folded(two[j])
            tang_ref[base + j] = (1.0 - h * h) * pre[
                :, half_lanes + j * 128 : half_lanes + (j + 1) * 128
            ] + folded(d_two[j])
        envelope = [env_ref[c, pl.ds(base, GROUP), :] for c in range(4)]
        for block in range(13):
            rows = slice(block * 8, block * 8 + 8)
            total = [mom_ref[c, rows, :] for c in range(4)]
            for j in range(GROUP):
                x = feat_ref[base + j, rows, :]
                for c in range(4):
                    total[c] = total[c] + envelope[c][j : j + 1, :] * x
            for c in range(4):
                mom_ref[c, rows, :] = total[c]
        return carry

    lax.fori_loop(0, SLOTS // GROUP, forward, 0)
    mom_ref[...] = mom_ref[...] * (1.0 / SLOTS)

    lead = [mom_ref[c, 0:16, :] for c in range(4)]
    for m in range(100):
        r = m // 25 * 24 + m % 25 if m % 25 < 24 else 96 + m // 25
        total = mom_ref[0, r : r + 1, :] * lead[0]
        for c in range(1, 4):
            total = total + mom_ref[c, r : r + 1, :] * lead[c]
        desc_ref[m * 16 : m * 16 + 16, :] = total

    fit1_copy.wait()
    weight = split(fit1_ref[...])
    high, low = split(desc_ref[...])
    hidden = dot(weight[0], jnp.concatenate([high, low], axis=1))
    hidden = hidden[:, 0:128] + (hidden[:, 128:256] + dot(weight[1], high))
    kind = type_ref[...]
    term = jnp.where(
        kind == 0,
        column(9, 0, 240),
        jnp.where(kind == 1, column(10, 0, 240), jnp.where(kind == 2, column(11, 0, 240), column(12, 0, 240))),
    )
    first = jnp.tanh(hidden + term)
    weight_2 = split(fit2_ref[...])
    second = jnp.tanh(dot3(weight_2, split(first)) + column(7, 0, 240))
    lane = lax.broadcasted_iota(jnp.int32, (1, 128), 1)
    own_live = jnp.where(lane < count_ref[0, 0], 1.0, 0.0)
    read = column(8, 0, 240)
    energy = jnp.sum(read * (first + second) * own_live, axis=(0, 1), keepdims=True)
    energy_ref[0, 0] = energy[0, 0]
    upper = read * own_live
    inner = upper * (1.0 - second * second)
    back = upper + dot3(weight_2, split(inner), ((0,), (0,)))
    back = back * (1.0 - first * first)
    flip_ref[...] = jnp.zeros((128, 256), F32)
    flip_ref[:, 0:240] = jnp.transpose(back)
    turned = dot3(split(flip_ref[:, 0:240]), weight)
    for part in range(12):
        desc_ref[part * 128 : (part + 1) * 128, :] = jnp.transpose(turned[:, part * 128 : (part + 1) * 128])
    desc_ref[1536:1600, :] = jnp.transpose(turned[:, 1536:1600])

    grad_mom_ref[...] = jnp.zeros((4, 104, 128), F32)
    gathered = [jnp.zeros((16, 128), F32) for _ in range(4)]
    for m in range(100):
        r = m // 25 * 24 + m % 25 if m % 25 < 24 else 96 + m // 25
        part = desc_ref[m * 16 : m * 16 + 16, :]
        for c in range(4):
            gathered[c] = gathered[c] + mom_ref[c, r : r + 1, :] * part
            grad_mom_ref[c, r : r + 1, :] = jnp.sum(part * lead[c], axis=0, keepdims=True)
    for c in range(4):
        grad_mom_ref[c, 0:16, :] = grad_mom_ref[c, 0:16, :] + gathered[c]
    grad_mom_ref[...] = grad_mom_ref[...] * (1.0 / SLOTS)

    step = 8

    def backward(group, carry):
        base = pl.multiple_of(group * step, step)
        value = [[jnp.zeros((8, 128), F32) for _ in range(4)] for _ in range(step)]
        slope = [[jnp.zeros((8, 128), F32) for _ in range(4)] for _ in range(step)]
        for ref, total in ((feat_ref, value), (tang_ref, slope)):
            for block in range(13):
                rows = slice(block * 8, block * 8 + 8)
                grads = [grad_mom_ref[c, rows, :] for c in range(4)]
                for j in range(step):
                    x = ref[base + j, rows, :]
                    for c in range(4):
                        total[j][c] = total[j][c] + grads[c] * x
        for j in range(step):
            through = jnp.zeros((8, 128), F32)
            for c in range(4):
                through = through + env_ref[c, pl.ds(base + j, 1), :] * slope[j][c]
                den_ref[c, pl.ds(base + j, 1), :] = jnp.sum(value[j][c], axis=0, keepdims=True)
            den_ref[4, pl.ds(base + j, 1), :] = jnp.sum(through, axis=0, keepdims=True)
        return carry

    lax.fori_loop(0, SLOTS // step, backward, 0)

    own = [jnp.zeros((8, 128), F32) for _ in range(3)]
    for group in range(SLOTS // 8):
        rows = slice(group * 8, group * 8 + 8)
        v = [pair_ref[c, rows, :] for c in range(3)]
        inverse = pair_ref[4, rows, :]
        scale = pair_ref[5, rows, :] * inverse * inverse * (1.0 / RANGE)
        by_v = [den_ref[c + 1, rows, :] for c in range(3)]
        along = v[0] * by_v[0] + v[1] * by_v[1] + v[2] * by_v[2]
        radial = inverse * (den_ref[0, rows, :] + den_ref[4, rows, :] + 2.0 * inverse * along)
        for c in range(3):
            grad = scale * (by_v[c] - v[c] * radial)
            pair_ref[c, rows, :] = grad
            own[c] = own[c] - grad
    own_rows = [jnp.sum(own[c], axis=0, keepdims=True) for c in range(3)]
    own_ref[...] = jnp.where(
        row8[0:4] == 0, own_rows[0], jnp.where(row8[0:4] == 1, own_rows[1], jnp.where(row8[0:4] == 2, own_rows[2], 0.0))
    )

    line = lax.broadcasted_iota(jnp.int32, (48, 128), 0)
    direction = line % 4
    domain = line // 12 + 3 * (line // 4 % 3)
    domain = jnp.where(line < 36, domain, -1)
    atom_index = lax.broadcasted_iota(jnp.int32, (128, 128), 0)

    def scatter(group, total):
        base = pl.multiple_of(group * GROUP, GROUP)
        entry = jnp.maximum(table_ref[pl.ds(base, GROUP), :], 0)
        block = entry >> 7
        atom = entry & (ATOMS - 1)
        grads = [pair_ref[c, pl.ds(base, GROUP), :] for c in range(3)]
        for j in range(GROUP):
            grad = jnp.where(
                direction == 0,
                grads[0][j : j + 1, :],
                jnp.where(direction == 1, grads[1][j : j + 1, :], grads[2][j : j + 1, :]),
            )
            grad = jnp.where((domain == block[j : j + 1, :]) & (direction < 3), grad, 0.0)
            high, low = split(grad)
            left_ref[0:48, j * 128 : (j + 1) * 128] = high
            left_ref[48:96, j * 128 : (j + 1) * 128] = low
            pick_ref[:, j * 128 : (j + 1) * 128] = jnp.where(atom_index == atom[j : j + 1, :], 1.0, 0.0).astype(BF16)
        return total + dot(left_ref[...], pick_ref[...], ((1,), (1,)))

    total = lax.fori_loop(0, SLOTS // GROUP, scatter, jnp.zeros((96, 128), F32))
    total = total[0:48] + total[48:96]
    for col, out in enumerate((out_low, out_mid, out_high)):
        for slab in range(3):
            start = col * 12 + slab * 4
            out[slab] = total[start : start + 4]


def call(kernel, outs, scratch, operands, name, flops, moved, smem=(), left=(), limit=60):
    vmem = pl.BlockSpec(memory_space=pltpu.VMEM)
    scalar = pl.BlockSpec(memory_space=pltpu.SMEM)
    anywhere = pl.BlockSpec(memory_space=pltpu.HBM)
    return pl.pallas_call(
        kernel,
        out_shape=[
            jax.ShapeDtypeStruct(*item) if isinstance(item[0], tuple) else jax.ShapeDtypeStruct(item, F32) for item in outs
        ],
        in_specs=[scalar if i in smem else anywhere if i in left else vmem for i in range(len(operands))],
        out_specs=[scalar if shape == (1, 1) else vmem for shape in outs],
        scratch_shapes=[pltpu.VMEM(*item) if isinstance(item, tuple) else item for item in scratch],
        name=name,
        cost_estimate=pl.CostEstimate(flops=flops, bytes_accessed=moved, transcendentals=0),
        compiler_params=pltpu.CompilerParams(vmem_limit_bytes=limit * 2**20),
    )(*operands)


def local(
    positions,
    atom_types,
    atom_counts,
    neighbours,
    centroid_owner_atoms,
    centroid_cell_offsets,
    emb_first,
    emb_second,
    emb_second_bias,
    emb_third,
    emb_third_bias,
    fit_first,
    fit_type,
    fit_second,
    fit_second_bias,
    fit_out,
):
    basis_h, basis_l, z_h, z_l, zt_h, zt_l, y_h, y_l, yt_h, yt_l = tables()
    pos = positions.reshape(3, 1, ATOMS)
    kinds = atom_types.reshape(1, ATOMS)
    count = atom_counts.reshape(1, 1)
    owner = centroid_owner_atoms.reshape(1, CENTRES)
    shift = centroid_cell_offsets.reshape(3, 1, CENTRES)
    index = (lax.axis_index("slab") * COLS + lax.axis_index("col")).reshape(1, 1)

    def ring(value, axis, step):
        size = lax.axis_size(axis)
        return lax.ppermute(value, axis, [(i, (i + step) % size) for i in range(size)])

    (packed,) = call(
        pack_kernel,
        [(1, 8, ATOMS)],
        [
            ((8, 256), F32),
            ((3, 1, ATOMS), F32),
            ((1, ATOMS), jnp.int32),
            ((1, CENTRES), jnp.int32),
            ((3, 1, CENTRES), F32),
            pltpu.SemaphoreType.DMA((4,)),
        ],
        [pos, kinds, owner, shift, count],
        "pack",
        1_000_000,
        10_000,
        (4,),
        range(4),
    )
    mid = jnp.concatenate([ring(packed, "slab", 1), packed, ring(packed, "slab", -1)], 0)
    low = ring(mid, "col", 1)
    high = ring(mid, "col", -1)

    (outgoing,) = call(
        spread_kernel,
        [(MESH, 1, CHUNK_IN)],
        [
            ((8, 512), F32),
            ((CELL_Z * PATCH_Y, 512), F32),
            ((CELL_Z * PATCH_Y, 512), F32),
            ((MESH, CHUNK_IN), F32),
        ],
        [mid, basis_h, basis_l],
        "spread",
        5_000_000_000,
        1_000_000,
    )
    outgoing, low, high = lax.optimization_barrier((outgoing, low, high))
    plane = lax.all_to_all(outgoing, BOTH, 0, 0, tiled=True)

    pairs = SLOTS * ATOMS
    short, own, back_mid, back_low, back_high = call(
        short_kernel,
        [(1, 1), (4, 128), (3, 4, 128), (3, 4, 128), (3, 4, 128)],
        [
            ((240, 1600), F32),
            pltpu.SemaphoreType.DMA(()),
            ((256, 128), F32),
            ((128, 256), F32),
            ((6, SLOTS, 128), F32),
            ((4, SLOTS, 128), F32),
            ((5, 32, 128), F32),
            ((128, 128), F32),
            ((256, 128), F32),
            ((64, 128), F32),
            ((104, 128), F32),
            ((96, 2 * GROUP * 128), BF16),
            ((192, 2 * GROUP * 128), BF16),
            ((SLOTS, 104, 128), F32),
            ((SLOTS, 104, 128), F32),
            ((4, 104, 128), F32),
            ((1600, 128), F32),
            ((4, 104, 128), F32),
            ((5, SLOTS, 128), F32),
            ((96, GROUP * 128), BF16),
            ((128, GROUP * 128), BF16),
        ],
        [
            neighbours.reshape(ATOMS, SLOTS).T,
            kinds,
            count,
            mid,
            low,
            high,
            emb_first.T,
            emb_second.T,
            emb_second_bias.reshape(1, -1),
            emb_third.T,
            emb_third_bias.reshape(1, -1),
            fit_first,
            fit_type.T,
            fit_second,
            fit_second_bias.reshape(1, -1),
            fit_out.reshape(1, -1),
        ],
        "short",
        pairs * 400_000,
        4_000_000,
        (2,),
        (11,),
    )

    (returning,) = call(
        solve_kernel,
        [(MESH, 1, CHUNK)],
        [((CHUNK // 128, MESH, 128), F32), ((PATCH_Z * SLABS, PATCH_Y * COLS), F32)],
        [plane, short, index, z_h, z_l, zt_h, zt_l, y_h, y_l, yt_h, yt_l],
        "solve",
        400_000_000,
        2_000_000,
        (1, 2),
        limit=40,
    )
    potential = lax.all_to_all(returning, BOTH, 0, 0, tiled=True)

    ghosts = back_mid + ring(back_low, "col", -1) + ring(back_high, "col", 1)
    ghosts, pos = lax.optimization_barrier((ghosts, pos))
    weights = call(
        weigh_kernel,
        [((MESH, 512), BF16), ((MESH, 512), BF16), (56, 256), (56, 256), (8, 256)],
        [((8, 256), F32)],
        [pos, kinds, count, owner, shift, basis_h, basis_l],
        "weigh",
        400_000_000,
        1_000_000,
        (2,),
        limit=40,
    )
    from_low, from_high = ring(ghosts[2], "slab", 1), ring(ghosts[0], "slab", -1)

    energy, atom_force, centre_force = call(
        interpolate_kernel,
        [(1, 128), (3, 1, ATOMS), (3, 1, CENTRES)],
        [((MESH, CHUNK), F32)],
        [potential, *weights, own, ghosts, from_low, from_high],
        "interpolate",
        600_000_000,
        1_500_000,
        limit=40,
    )
    return energy[0, 0], atom_force.reshape(1, 1, 3, ATOMS), centre_force.reshape(1, 1, 3, CENTRES)


def solution(mesh):
    return jax.shard_map(
        local,
        mesh=mesh,
        in_specs=(
            P("slab", "col", None, None),
            P("slab", "col", None),
            P("slab", "col"),
            P("slab", "col", None, None),
            P("slab", "col", None),
            P("slab", "col", None, None),
            P(),
            P(),
            P(),
            P(),
            P(),
            P(),
            P(),
            P(),
            P(),
            P(),
        ),
        out_specs=(P(), P("slab", "col", None, None), P("slab", "col", None, None)),
        check_vma=False,
    )
```

```python
import functools
import math

import jax
import jax.numpy as jnp
import ml_dtypes
import numpy as np
from jax import lax
from jax.experimental import pallas as pl
from jax.experimental.pallas import tpu as pltpu
from jax.sharding import PartitionSpec as P

CHARGES = (6.0, 1.0, 1.0, -1.0)
WANNIER = -8.0
RANGE = 24.0
COUPLING = 0.05
SMEAR = 0.6
ATOMS = 128
CENTRES = 32
SLOTS = 64
MESH = 256
SLABS, COLS = 32, 8
CELL_Z, CELL_Y = 8, 32
REACH = 3
PATCH_Z, PATCH_Y = 14, 40
PATCH = PATCH_Z * PATCH_Y
CHUNK_IN = 384
CHUNK = 640
GROUP = 16
F32 = jnp.float32
BF16 = jnp.bfloat16
BOTH = ("slab", "col")


def halves(array):
    high = array.astype(ml_dtypes.bfloat16)
    low = (array - high.astype(np.float64)).astype(ml_dtypes.bfloat16)
    return high, low


@functools.lru_cache(maxsize=None)
def tables():
    k = np.arange(MESH)[:, None]
    n = np.arange(MESH)[None, :]
    phase = 2.0 * np.pi * ((k * n) % MESH) / MESH
    basis = np.where(k <= MESH // 2, np.cos(phase), np.sin(phase)) * math.sqrt(2.0 / MESH)
    basis[0] = 1.0 / math.sqrt(MESH)
    basis[MESH // 2] = np.where(np.arange(MESH) % 2 == 0, 1.0, -1.0) / math.sqrt(MESH)
    cells_z = (np.arange(PATCH_Z)[:, None] - REACH + CELL_Z * np.arange(SLABS)[None, :]) % MESH
    along_z = basis[:, cells_z.reshape(-1)]
    cells_z = (np.arange(CELL_Z)[:, None] + CELL_Z * np.arange(SLABS)[None, :]) % MESH
    inside_z = basis[:, cells_z.reshape(-1)]
    cells_y = (np.arange(PATCH_Y)[None, :] - REACH + CELL_Y * np.arange(COLS)[:, None]) % MESH
    along_y = basis[:, cells_y.reshape(-1)].T
    out = []
    for matrix in (basis, inside_z, along_z.T, along_y, along_y.T):
        out.extend(halves(matrix))
    return out


def split(value):
    high = value.astype(BF16)
    return high, (value - high.astype(F32)).astype(BF16)


def dot(left, right, dims=((1,), (0,))):
    return lax.dot_general(left, right, (dims, ((), ())), preferred_element_type=F32)


def dot3(left, right, dims=((1,), (0,))):
    if dims != ((1,), (0,)) or left[0].shape[0] % 16:
        return dot(left[0], right[0], dims) + (dot(left[0], right[1], dims) + dot(left[1], right[0], dims))
    rows = left[0].shape[0]
    both = dot(jnp.concatenate(left, axis=0), right[0])
    return both[0:rows] + (both[rows:] + dot(left[0], right[1]))


def lanes(table, index):
    return jnp.take_along_axis(table, index, axis=1)


def spline(z, slope):
    a = jnp.abs(z)
    a2 = z * z
    rest = 2.5 - a
    rest2 = rest * rest
    inner = 115.0 / 192.0 + a2 * (-0.625 + 0.25 * a2)
    middle = (55.0 + a * (20.0 + a * (-120.0 + a * (80.0 - 16.0 * a)))) * (1.0 / 96.0)
    outer = rest2 * rest2 * (1.0 / 24.0)
    near, mid, far = a < 0.5, a < 1.5, a < 2.5
    value = jnp.where(near, inner, jnp.where(mid, middle, jnp.where(far, outer, 0.0)))
    if not slope:
        return value, None
    d_inner = a * (a2 - 1.25)
    d_middle = (20.0 + a * (-240.0 + a * (240.0 - 64.0 * a))) * (1.0 / 96.0)
    d_outer = rest2 * rest * (-1.0 / 6.0)
    d = jnp.where(near, d_inner, jnp.where(mid, d_middle, jnp.where(far, d_outer, 0.0)))
    return value, jnp.where(z < 0.0, -d, d)


def points(pos_ref, type_ref, count_ref, owner_ref, shift_ref, place_ref):
    lane = lax.broadcasted_iota(jnp.int32, (8, 128), 1)
    place_ref[...] = jnp.zeros((8, 256), F32)
    place_ref[0:3, 0:128] = pos_ref[:, 0, :]
    place_ref[0:3, 128:160] = shift_ref[:, 0, :]
    place_ref[3:4, 128:160] = owner_ref[...].astype(F32)
    row = lax.broadcasted_iota(jnp.int32, (8, 128), 0)
    extent = jnp.where(row == 0, float(MESH), jnp.where(row == 1, float(CELL_Y), float(CELL_Z)))
    atoms = place_ref[:, 0:128] * extent
    owner = jnp.where(lane < CENTRES, place_ref[3:4, 128:256].astype(jnp.int32), -1)
    carrying = jnp.broadcast_to(jnp.maximum(owner, 0), (8, 128))
    centres = lanes(atoms, carrying) + place_ref[:, 128:256]
    kind = type_ref[...]
    charge = jnp.where(
        kind == 0, CHARGES[0], jnp.where(kind == 1, CHARGES[1], jnp.where(kind == 2, CHARGES[2], CHARGES[3]))
    )
    charge = jnp.where(lane[0:1] < count_ref[0, 0], charge, 0.0)
    centre_charge = jnp.where(owner[0:1] >= 0, WANNIER, 0.0)
    place_ref[:, 0:128] = atoms
    place_ref[:, 128:256] = centres
    return jnp.concatenate([charge, centre_charge], axis=1), owner[0:1]


def offsets(coordinate, cells, low):
    cell = lax.broadcasted_iota(jnp.int32, (cells, coordinate.shape[1]), 0) + low
    return coordinate - cell.astype(F32) - 0.5


def wrapped(z):
    return z - float(MESH) * jnp.round(z * (1.0 / MESH))


def pack_kernel(*refs):
    sources, (count_ref, out_ref, place_ref), copies, sems = refs[:4], refs[4:7], refs[7:11], refs[11]
    moves = [pltpu.make_async_copy(a, b, sems.at[i]) for i, (a, b) in enumerate(zip(sources, copies))]
    for move in moves:
        move.start()
    for move in moves:
        move.wait()
    pos_ref, type_ref, owner_ref, shift_ref = copies
    charge, _ = points(pos_ref, type_ref, count_ref, owner_ref, shift_ref, place_ref)
    out_ref[0] = jnp.zeros((8, 128), F32)
    out_ref[0, 0:3, :] = place_ref[0:3, 0:128]
    out_ref[0, 3:4, :] = type_ref[...].astype(F32)
    out_ref[0, 4:5, :] = charge[:, 0:128]
    for c in range(3):
        out_ref[0, 5:6, c * 32 : c * 32 + 32] = place_ref[c : c + 1, 128:160]
    out_ref[0, 5:6, 96:128] = charge[:, 128:160]


def spread_kernel(mid_ref, basis_h, basis_l, out_ref, place_ref, amp_h, amp_l, all_ref):
    place_ref[...] = jnp.zeros((8, 512), F32)
    for d in range(3):
        shift = (0.0, 0.0, float((d - 1) * CELL_Z), 0.0)
        for c, row in enumerate((0, 1, 2, 4)):
            place_ref[c : c + 1, d * 128 : d * 128 + 128] = mid_ref[d, row : row + 1, :] + shift[c]
            place_ref[c : c + 1, 384 + d * 32 : 416 + d * 32] = mid_ref[d, 5:6, c * 32 : c * 32 + 32] + shift[c]
    along_x, _ = spline(wrapped(offsets(place_ref[0:1, :], MESH, 0)), False)
    along_y, _ = spline(offsets(place_ref[1:2, :], PATCH_Y, -REACH), False)
    along_z, _ = spline(offsets(place_ref[2:3, :], CELL_Z, 0), False)
    along_z = along_z * place_ref[3:4, :]
    for cell in range(CELL_Z):
        block = along_z[cell : cell + 1, :] * along_y
        high = block.astype(BF16).astype(F32)
        amp_h[cell * PATCH_Y : (cell + 1) * PATCH_Y, :] = high
        amp_l[cell * PATCH_Y : (cell + 1) * PATCH_Y, :] = block - high
    spectral = split(dot3((basis_h[...], basis_l[...]), split(along_x)))
    all_ref[...] = jnp.zeros((MESH, CHUNK_IN), F32)
    all_ref[:, 0 : CELL_Z * PATCH_Y] = dot3(
        spectral, (amp_h[...].astype(BF16), amp_l[...].astype(BF16)), ((1,), (1,))
    )
    out_ref[:, 0, :] = all_ref[...]


def solve_kernel(
    plane_ref, short_ref, z_h, z_l, zt_h, zt_l, y_h, y_l, yt_h, yt_l, out_ref, all_ref, grid_ref
):
    for tile in range(CHUNK_IN // 128):
        all_ref[tile] = plane_ref[:, 0, tile * 128 : (tile + 1) * 128]
    for col in range(COLS):
        rows = jnp.concatenate(
            [all_ref[tile, pl.ds(col, SLABS, stride=COLS), :] for tile in range(CHUNK_IN // 128)], axis=1
        )
        for cell in range(CELL_Z):
            grid_ref[cell * SLABS : (cell + 1) * SLABS, col * PATCH_Y : (col + 1) * PATCH_Y] = rows[
                :, cell * PATCH_Y : (cell + 1) * PATCH_Y
            ]
    by_y = dot3(split(grid_ref[0 : CELL_Z * SLABS, :]), (y_h[...], y_l[...]))
    spectrum = dot3((z_h[...], z_l[...]), split(by_y))
    unit = 2.0 * math.pi / MESH
    index_z = lax.broadcasted_iota(jnp.int32, (MESH, MESH), 0)
    index_y = lax.broadcasted_iota(jnp.int32, (MESH, MESH), 1)
    index_x = jnp.full((MESH, MESH), lax.axis_index("slab") * COLS + lax.axis_index("col"), jnp.int32)

    def square_of(index):
        wave = jnp.minimum(index, MESH - index).astype(F32) * unit
        return wave * wave

    square = square_of(index_z) + square_of(index_y) + square_of(index_x)
    nonzero = square > 0.0
    safe = jnp.where(nonzero, square, 1.0)
    green = jnp.where(nonzero, 4.0 * math.pi * jnp.exp(-0.5 * SMEAR * SMEAR * square) / safe, 0.0)
    filtered = spectrum * green
    energy = 0.5 * COUPLING * jnp.sum(spectrum * filtered, axis=(0, 1), keepdims=True)
    energy = energy + short_ref[0, 0]
    back_z = dot3((zt_h[...], zt_l[...]), split(filtered))
    grid_ref[...] = dot3(split(back_z), (yt_h[...], yt_l[...]))
    tail = jnp.broadcast_to(energy, (SLABS, CHUNK - PATCH))
    for col in range(COLS):
        pieces = [
            grid_ref[cell * SLABS : (cell + 1) * SLABS, col * PATCH_Y : (col + 1) * PATCH_Y]
            for cell in range(PATCH_Z)
        ]
        rows = jnp.concatenate(pieces + [tail], axis=1)
        for tile in range(CHUNK // 128):
            all_ref[tile, pl.ds(col, SLABS, stride=COLS), :] = rows[:, tile * 128 : (tile + 1) * 128]
    for tile in range(CHUNK // 128):
        out_ref[:, 0, tile * 128 : (tile + 1) * 128] = all_ref[tile]


def weigh_kernel(
    pos_ref,
    type_ref,
    count_ref,
    owner_ref,
    shift_ref,
    basis_h,
    basis_l,
    spectral_h,
    spectral_l,
    along_ref,
    slope_ref,
    point_ref,
    place_ref,
):
    charge, owner = points(pos_ref, type_ref, count_ref, owner_ref, shift_ref, place_ref)
    basis = (basis_h[...], basis_l[...])
    along_x, slope_x = spline(wrapped(offsets(place_ref[0:1, :], MESH, 0)), True)
    for start, weight in ((0, along_x), (256, slope_x)):
        high, low = split(dot3(basis, split(weight)))
        spectral_h[:, start : start + 256] = high
        spectral_l[:, start : start + 256] = low
    along_ref[0:PATCH_Y, :], slope_ref[0:PATCH_Y, :] = spline(offsets(place_ref[1:2, :], PATCH_Y, -REACH), True)
    along_ref[PATCH_Y:56, :], slope_ref[PATCH_Y:56, :] = spline(offsets(place_ref[2:3, :], 16, -REACH), True)
    point_ref[...] = jnp.zeros((8, 256), F32)
    point_ref[0:1, :] = -COUPLING * charge
    point_ref[1:2, 0:128] = owner.astype(F32)


def interpolate_kernel(
    back_ref,
    spectral_h,
    spectral_l,
    along_ref,
    slope_ref,
    point_ref,
    own_ref,
    kept_ref,
    from_low,
    from_high,
    energy_ref,
    atom_ref,
    centre_ref,
    all_ref,
):
    along_y, along_z = along_ref[0:PATCH_Y, :], along_ref[PATCH_Y:56, :]
    slope_y, slope_z = slope_ref[0:PATCH_Y, :], slope_ref[PATCH_Y:56, :]
    owner = point_ref[1:2, 0:128].astype(jnp.int32)
    all_ref[...] = back_ref[:, 0, :]
    energy_ref[...] = jnp.broadcast_to(
        jnp.sum(all_ref[:, PATCH : PATCH + 1], axis=(0, 1), keepdims=True)
        * (1.0 / (ATOMS * SLABS * COLS)),
        (1, 128),
    )
    turned = split(jnp.transpose(all_ref[...])[0:PATCH, :])
    both = dot3(turned, (spectral_h[...], spectral_l[...]))
    values, slopes = both[:, 0:256], both[:, 256:512]
    by_x = jnp.zeros((PATCH_Y, 256), F32)
    by_y = jnp.zeros((PATCH_Y, 256), F32)
    by_z = jnp.zeros((PATCH_Y, 256), F32)
    for cell in range(PATCH_Z):
        part = values[cell * PATCH_Y : (cell + 1) * PATCH_Y, :]
        by_x = by_x + along_z[cell : cell + 1, :] * slopes[cell * PATCH_Y : (cell + 1) * PATCH_Y, :]
        by_y = by_y + along_z[cell : cell + 1, :] * part
        by_z = by_z + slope_z[cell : cell + 1, :] * part
    scale = point_ref[0:1, :]
    force_x = jnp.sum(along_y * by_x, axis=0, keepdims=True) * scale
    force_y = jnp.sum(slope_y * by_y, axis=0, keepdims=True) * scale
    force_z = jnp.sum(along_y * by_z, axis=0, keepdims=True) * scale
    row = lax.broadcasted_iota(jnp.int32, (8, 256), 0)
    force = jnp.where(
        row == 0, force_x, jnp.where(row == 1, force_y, jnp.where(row == 2, force_z, 0.0))
    )
    atom_index = lax.broadcasted_iota(jnp.int32, (128, 128), 0)
    picker = jnp.where(atom_index == owner, 1.0, 0.0).astype(BF16)
    centre = force[:, 128:256]
    high, low = split(centre)
    lower = (centre - high.astype(F32) - low.astype(F32)).astype(BF16)
    dims = ((1,), (1,))
    carried = dot(high, picker, dims) + (dot(low, picker, dims) + dot(lower, picker, dims))
    short = (own_ref[...] + kept_ref[1]) + (from_low[...] + from_high[...])
    atom_ref[:, 0, :] = force[0:3, 0:128] + carried[0:3] - short[0:3]
    centre_ref[:, 0, :] = force[0:3, 128:160]


def short_kernel(
    table_ref,
    type_ref,
    count_ref,
    mid_ref,
    low_ref,
    high_ref,
    emb1_ref,
    emb2_ref,
    bias2_ref,
    emb3_ref,
    bias3_ref,
    fit1_hbm,
    fit_type_ref,
    fit2_ref,
    fit_bias_ref,
    fit_out_ref,
    energy_ref,
    own_ref,
    out_mid,
    out_low,
    out_high,
    fit1_ref,
    fit1_sem,
    turn_ref,
    flip_ref,
    pair_ref,
    env_ref,
    first_ref,
    second_ref,
    third_ref,
    bias2_s,
    bias3_s,
    in2_ref,
    in3_ref,
    feat_ref,
    tang_ref,
    mom_ref,
    desc_ref,
    grad_mom_ref,
    den_ref,
    left_ref,
    pick_ref,
):
    ghost_refs = (low_ref, mid_ref, high_ref)
    fit1_copy = pltpu.make_async_copy(fit1_hbm, fit1_ref, fit1_sem)
    fit1_copy.start()
    centre = [mid_ref[1, c : c + 1, :] for c in range(3)]

    for group in range(SLOTS // 8):
        rows = slice(group * 8, group * 8 + 8)
        entry = table_ref[rows, :]
        live = jnp.where(entry >= 0, 1.0, 0.0)
        entry = jnp.maximum(entry, 0)
        block = entry >> 7
        atom = entry & (ATOMS - 1)
        near = [jnp.zeros((8, 128), F32) for _ in range(4)]
        for b in range(9):
            ghost = ghost_refs[b % 3]
            here = block == b
            for c in range(4):
                line = ghost[b // 3, c : c + 1, :]
                if c == 1:
                    line = line + float((b % 3 - 1) * CELL_Y)
                if c == 2:
                    line = line + float((b // 3 - 1) * CELL_Z)
                near[c] = jnp.where(here, lanes(jnp.broadcast_to(line, (8, 128)), atom), near[c])
        v = [(near[c] - centre[c]) * (1.0 / RANGE) for c in range(3)]
        inverse = 1.0 / jnp.sqrt(1.0 + (v[0] * v[0] + v[1] * v[1] + v[2] * v[2]))
        for c in range(3):
            pair_ref[c, rows, :] = v[c]
            env_ref[c + 1, rows, :] = live * v[c] * inverse * inverse
        pair_ref[3, rows, :] = near[3]
        pair_ref[4, rows, :] = inverse
        pair_ref[5, rows, :] = live
        env_ref[0, rows, :] = live * inverse

    flip_ref[...] = jnp.zeros((128, 256), F32)
    flip_ref[0:5, 0:25] = emb1_ref[...]
    flip_ref[5:6, 0:50] = bias2_ref[...]
    flip_ref[6:7, 0:100] = bias3_ref[...]
    flip_ref[7:8, 0:240] = fit_bias_ref[...]
    flip_ref[8:9, 0:240] = fit_out_ref[...]
    flip_ref[9:13, 0:240] = fit_type_ref[...]
    turn_ref[...] = jnp.transpose(flip_ref[...])

    def column(at, start, stop):
        return jnp.broadcast_to(turn_ref[start:stop, at : at + 1], (stop - start, 128))

    first_ref[...] = jnp.zeros((5, 32, 128), F32)
    for c in range(5):
        first_ref[c, 0:25, :] = column(c, 0, 25)
    bias2_s[...] = jnp.zeros((64, 128), F32)
    for half in range(2):
        bias2_s[half * 32 : half * 32 + 25, :] = column(5, half * 25, half * 25 + 25)
    bias3_s[...] = jnp.zeros((104, 128), F32)
    for quarter in range(4):
        bias3_s[quarter * 24 : quarter * 24 + 24, :] = column(6, quarter * 25, quarter * 25 + 24)
        bias3_s[96 + quarter : 97 + quarter, :] = column(6, quarter * 25 + 24, quarter * 25 + 25)
    second_ref[...] = jnp.zeros((128, 128), F32)
    third_ref[...] = jnp.zeros((256, 128), F32)
    for half in range(2):
        block = emb2_ref[:, half * 25 : half * 25 + 25]
        high = block.astype(BF16).astype(F32)
        for stack, part in enumerate((high, high, block - high)):
            second_ref[stack * 32 : stack * 32 + 25, half * 32 : half * 32 + 25] = part
    for quarter in range(4):
        for half in range(2):
            block = emb3_ref[half * 25 : half * 25 + 25, quarter * 25 : quarter * 25 + 25]
            high = block.astype(BF16).astype(F32)
            for stack, part in enumerate((high, high, block - high)):
                start = stack * 64 + half * 32
                third_ref[start : start + 25, quarter * 24 : quarter * 24 + 24] = part[:, 0:24]
                third_ref[start : start + 25, 96 + quarter : 97 + quarter] = part[:, 24:25]
    weight2 = jnp.transpose(second_ref[...])[0:64, 0:96].astype(BF16)
    weight3 = jnp.transpose(third_ref[...])[0:104, 0:192].astype(BF16)
    mom_ref[...] = jnp.zeros((4, 104, 128), F32)
    half_lanes = GROUP * 128
    row8 = lax.broadcasted_iota(jnp.int32, (8, 128), 0)

    def forward(group, carry):
        base = pl.multiple_of(group * GROUP, GROUP)
        smooth = env_ref[0, pl.ds(base, GROUP), :]
        kinds = pair_ref[3, pl.ds(base, GROUP), :]
        slope_row = first_ref[0]
        one, d_one = [], []
        for j in range(GROUP):
            s = smooth[j : j + 1, :]
            kind = kinds[j : j + 1, :]
            term = jnp.where(
                kind == 0.0,
                first_ref[1],
                jnp.where(kind == 1.0, first_ref[2], jnp.where(kind == 2.0, first_ref[3], first_ref[4])),
            )
            x = jnp.tanh(slope_row * s + term)
            d = (1.0 - x * x) * slope_row
            for value, start in ((x, j * 128), (d, half_lanes + j * 128)):
                high, low = split(value)
                in2_ref[0:32, start : start + 128] = high
                in2_ref[32:64, start : start + 128] = low
                in2_ref[64:96, start : start + 128] = high
            one.append(x)
            d_one.append(d)
        pre = dot(weight2, in2_ref[...])
        two, d_two = [], []
        for j in range(GROUP):
            h = jnp.tanh(pre[:, j * 128 : (j + 1) * 128] + bias2_s[...])
            x = h + jnp.concatenate([one[j], one[j]], axis=0)
            d = (1.0 - h * h) * pre[
                :, half_lanes + j * 128 : half_lanes + (j + 1) * 128
            ] + jnp.concatenate([d_one[j], d_one[j]], axis=0)
            for value, start in ((x, j * 128), (d, half_lanes + j * 128)):
                high, low = split(value)
                in3_ref[0:64, start : start + 128] = high
                in3_ref[64:128, start : start + 128] = low
                in3_ref[128:192, start : start + 128] = high
            two.append(x)
            d_two.append(d)
        pre = dot(weight3, in3_ref[...])

        def folded(value):
            last = jnp.where(row8 < 4, jnp.where(row8 % 2 == 0, value[24:25], value[56:57]), 0.0)
            return jnp.concatenate([value[0:24], value[32:56], value[0:24], value[32:56], last], axis=0)

        for j in range(GROUP):
            h = jnp.tanh(pre[:, j * 128 : (j + 1) * 128] + bias3_s[...])
            feat_ref[base + j] = h + folded(two[j])
            tang_ref[base + j] = (1.0 - h * h) * pre[
                :, half_lanes + j * 128 : half_lanes + (j + 1) * 128
            ] + folded(d_two[j])
        envelope = [env_ref[c, pl.ds(base, GROUP), :] for c in range(4)]
        for block in range(13):
            rows = slice(block * 8, block * 8 + 8)
            total = [mom_ref[c, rows, :] for c in range(4)]
            for j in range(GROUP):
                x = feat_ref[base + j, rows, :]
                for c in range(4):
                    total[c] = total[c] + envelope[c][j : j + 1, :] * x
            for c in range(4):
                mom_ref[c, rows, :] = total[c]
        return carry

    lax.fori_loop(0, SLOTS // GROUP, forward, 0)
    mom_ref[...] = mom_ref[...] * (1.0 / SLOTS)

    lead = [mom_ref[c, 0:16, :] for c in range(4)]
    for m in range(100):
        r = m // 25 * 24 + m % 25 if m % 25 < 24 else 96 + m // 25
        total = mom_ref[0, r : r + 1, :] * lead[0]
        for c in range(1, 4):
            total = total + mom_ref[c, r : r + 1, :] * lead[c]
        desc_ref[m * 16 : m * 16 + 16, :] = total

    fit1_copy.wait()
    weight = split(fit1_ref[...])
    high, low = split(desc_ref[...])
    hidden = dot(weight[0], jnp.concatenate([high, low], axis=1))
    hidden = hidden[:, 0:128] + (hidden[:, 128:256] + dot(weight[1], high))
    kind = type_ref[...]
    term = jnp.where(
        kind == 0,
        column(9, 0, 240),
        jnp.where(kind == 1, column(10, 0, 240), jnp.where(kind == 2, column(11, 0, 240), column(12, 0, 240))),
    )
    first = jnp.tanh(hidden + term)
    weight_2 = split(fit2_ref[...])
    second = jnp.tanh(dot3(weight_2, split(first)) + column(7, 0, 240))
    lane = lax.broadcasted_iota(jnp.int32, (1, 128), 1)
    own_live = jnp.where(lane < count_ref[0, 0], 1.0, 0.0)
    read = column(8, 0, 240)
    energy = jnp.sum(read * (first + second) * own_live, axis=(0, 1), keepdims=True)
    energy_ref[0, 0] = energy[0, 0]
    upper = read * own_live
    inner = upper * (1.0 - second * second)
    back = upper + dot3(weight_2, split(inner), ((0,), (0,)))
    back = back * (1.0 - first * first)
    flip_ref[...] = jnp.zeros((128, 256), F32)
    flip_ref[:, 0:240] = jnp.transpose(back)
    turned = dot3(split(flip_ref[:, 0:240]), weight)
    for part in range(12):
        desc_ref[part * 128 : (part + 1) * 128, :] = jnp.transpose(turned[:, part * 128 : (part + 1) * 128])
    desc_ref[1536:1600, :] = jnp.transpose(turned[:, 1536:1600])

    grad_mom_ref[...] = jnp.zeros((4, 104, 128), F32)
    gathered = [jnp.zeros((16, 128), F32) for _ in range(4)]
    for m in range(100):
        r = m // 25 * 24 + m % 25 if m % 25 < 24 else 96 + m // 25
        part = desc_ref[m * 16 : m * 16 + 16, :]
        for c in range(4):
            gathered[c] = gathered[c] + mom_ref[c, r : r + 1, :] * part
            grad_mom_ref[c, r : r + 1, :] = jnp.sum(part * lead[c], axis=0, keepdims=True)
    for c in range(4):
        grad_mom_ref[c, 0:16, :] = grad_mom_ref[c, 0:16, :] + gathered[c]
    grad_mom_ref[...] = grad_mom_ref[...] * (1.0 / SLOTS)

    step = 8

    def backward(group, carry):
        base = pl.multiple_of(group * step, step)
        value = [[jnp.zeros((8, 128), F32) for _ in range(4)] for _ in range(step)]
        slope = [[jnp.zeros((8, 128), F32) for _ in range(4)] for _ in range(step)]
        for ref, total in ((feat_ref, value), (tang_ref, slope)):
            for block in range(13):
                rows = slice(block * 8, block * 8 + 8)
                grads = [grad_mom_ref[c, rows, :] for c in range(4)]
                for j in range(step):
                    x = ref[base + j, rows, :]
                    for c in range(4):
                        total[j][c] = total[j][c] + grads[c] * x
        for j in range(step):
            through = jnp.zeros((8, 128), F32)
            for c in range(4):
                through = through + env_ref[c, pl.ds(base + j, 1), :] * slope[j][c]
                den_ref[c, pl.ds(base + j, 1), :] = jnp.sum(value[j][c], axis=0, keepdims=True)
            den_ref[4, pl.ds(base + j, 1), :] = jnp.sum(through, axis=0, keepdims=True)
        return carry

    lax.fori_loop(0, SLOTS // step, backward, 0)

    own = [jnp.zeros((8, 128), F32) for _ in range(3)]
    for group in range(SLOTS // 8):
        rows = slice(group * 8, group * 8 + 8)
        v = [pair_ref[c, rows, :] for c in range(3)]
        inverse = pair_ref[4, rows, :]
        scale = pair_ref[5, rows, :] * inverse * inverse * (1.0 / RANGE)
        by_v = [den_ref[c + 1, rows, :] for c in range(3)]
        along = v[0] * by_v[0] + v[1] * by_v[1] + v[2] * by_v[2]
        radial = inverse * (den_ref[0, rows, :] + den_ref[4, rows, :] + 2.0 * inverse * along)
        for c in range(3):
            grad = scale * (by_v[c] - v[c] * radial)
            pair_ref[c, rows, :] = grad
            own[c] = own[c] - grad
    own_rows = [jnp.sum(own[c], axis=0, keepdims=True) for c in range(3)]
    own_ref[...] = jnp.where(
        row8[0:4] == 0, own_rows[0], jnp.where(row8[0:4] == 1, own_rows[1], jnp.where(row8[0:4] == 2, own_rows[2], 0.0))
    )

    line = lax.broadcasted_iota(jnp.int32, (48, 128), 0)
    direction = line % 4
    domain = line // 12 + 3 * (line // 4 % 3)
    domain = jnp.where(line < 36, domain, -1)
    atom_index = lax.broadcasted_iota(jnp.int32, (128, 128), 0)

    def scatter(group, total):
        base = pl.multiple_of(group * GROUP, GROUP)
        entry = jnp.maximum(table_ref[pl.ds(base, GROUP), :], 0)
        block = entry >> 7
        atom = entry & (ATOMS - 1)
        grads = [pair_ref[c, pl.ds(base, GROUP), :] for c in range(3)]
        for j in range(GROUP):
            grad = jnp.where(
                direction == 0,
                grads[0][j : j + 1, :],
                jnp.where(direction == 1, grads[1][j : j + 1, :], grads[2][j : j + 1, :]),
            )
            grad = jnp.where((domain == block[j : j + 1, :]) & (direction < 3), grad, 0.0)
            high, low = split(grad)
            left_ref[0:48, j * 128 : (j + 1) * 128] = high
            left_ref[48:96, j * 128 : (j + 1) * 128] = low
            pick_ref[:, j * 128 : (j + 1) * 128] = jnp.where(atom_index == atom[j : j + 1, :], 1.0, 0.0).astype(BF16)
        return total + dot(left_ref[...], pick_ref[...], ((1,), (1,)))

    total = lax.fori_loop(0, SLOTS // GROUP, scatter, jnp.zeros((96, 128), F32))
    total = total[0:48] + total[48:96]
    for col, out in enumerate((out_low, out_mid, out_high)):
        for slab in range(3):
            start = col * 12 + slab * 4
            out[slab] = total[start : start + 4]


def call(kernel, outs, scratch, operands, name, flops, moved, smem=(), left=(), limit=60):
    vmem = pl.BlockSpec(memory_space=pltpu.VMEM)
    scalar = pl.BlockSpec(memory_space=pltpu.SMEM)
    anywhere = pl.BlockSpec(memory_space=pltpu.HBM)
    return pl.pallas_call(
        kernel,
        out_shape=[
            jax.ShapeDtypeStruct(*item) if isinstance(item[0], tuple) else jax.ShapeDtypeStruct(item, F32) for item in outs
        ],
        in_specs=[scalar if i in smem else anywhere if i in left else vmem for i in range(len(operands))],
        out_specs=[scalar if shape == (1, 1) else vmem for shape in outs],
        scratch_shapes=[pltpu.VMEM(*item) if isinstance(item, tuple) else item for item in scratch],
        name=name,
        cost_estimate=pl.CostEstimate(flops=flops, bytes_accessed=moved, transcendentals=0),
        compiler_params=pltpu.CompilerParams(vmem_limit_bytes=limit * 2**20),
    )(*operands)


def local(
    positions,
    atom_types,
    atom_counts,
    neighbours,
    centroid_owner_atoms,
    centroid_cell_offsets,
    emb_first,
    emb_second,
    emb_second_bias,
    emb_third,
    emb_third_bias,
    fit_first,
    fit_type,
    fit_second,
    fit_second_bias,
    fit_out,
):
    basis_h, basis_l, z_h, z_l, zt_h, zt_l, y_h, y_l, yt_h, yt_l = tables()
    pos = positions.reshape(3, 1, ATOMS)
    kinds = atom_types.reshape(1, ATOMS)
    count = atom_counts.reshape(1, 1)
    owner = centroid_owner_atoms.reshape(1, CENTRES)
    shift = centroid_cell_offsets.reshape(3, 1, CENTRES)

    def ring(value, axis, step):
        size = lax.axis_size(axis)
        return lax.ppermute(value, axis, [(i, (i + step) % size) for i in range(size)])

    (packed,) = call(
        pack_kernel,
        [(1, 8, ATOMS)],
        [
            ((8, 256), F32),
            ((3, 1, ATOMS), F32),
            ((1, ATOMS), jnp.int32),
            ((1, CENTRES), jnp.int32),
            ((3, 1, CENTRES), F32),
            pltpu.SemaphoreType.DMA((4,)),
        ],
        [pos, kinds, owner, shift, count],
        "pack",
        1_000_000,
        10_000,
        (4,),
        range(4),
    )
    mid = jnp.concatenate([ring(packed, "slab", 1), packed, ring(packed, "slab", -1)], 0)
    low = ring(mid, "col", 1)
    high = ring(mid, "col", -1)

    (outgoing,) = call(
        spread_kernel,
        [(MESH, 1, CHUNK_IN)],
        [
            ((8, 512), F32),
            ((CELL_Z * PATCH_Y, 512), F32),
            ((CELL_Z * PATCH_Y, 512), F32),
            ((MESH, CHUNK_IN), F32),
        ],
        [mid, basis_h, basis_l],
        "spread",
        5_000_000_000,
        1_000_000,
    )
    outgoing, low, high = lax.optimization_barrier((outgoing, low, high))
    plane = lax.all_to_all(outgoing, BOTH, 0, 0, tiled=True)

    pairs = SLOTS * ATOMS
    short, own, back_mid, back_low, back_high = call(
        short_kernel,
        [(1, 1), (4, 128), (3, 4, 128), (3, 4, 128), (3, 4, 128)],
        [
            ((240, 1600), F32),
            pltpu.SemaphoreType.DMA(()),
            ((256, 128), F32),
            ((128, 256), F32),
            ((6, SLOTS, 128), F32),
            ((4, SLOTS, 128), F32),
            ((5, 32, 128), F32),
            ((128, 128), F32),
            ((256, 128), F32),
            ((64, 128), F32),
            ((104, 128), F32),
            ((96, 2 * GROUP * 128), BF16),
            ((192, 2 * GROUP * 128), BF16),
            ((SLOTS, 104, 128), F32),
            ((SLOTS, 104, 128), F32),
            ((4, 104, 128), F32),
            ((1600, 128), F32),
            ((4, 104, 128), F32),
            ((5, SLOTS, 128), F32),
            ((96, GROUP * 128), BF16),
            ((128, GROUP * 128), BF16),
        ],
        [
            neighbours.reshape(ATOMS, SLOTS).T,
            kinds,
            count,
            mid,
            low,
            high,
            emb_first.T,
            emb_second.T,
            emb_second_bias.reshape(1, -1),
            emb_third.T,
            emb_third_bias.reshape(1, -1),
            fit_first,
            fit_type.T,
            fit_second,
            fit_second_bias.reshape(1, -1),
            fit_out.reshape(1, -1),
        ],
        "short",
        pairs * 400_000,
        4_000_000,
        (2,),
        (11,),
    )

    (returning,) = call(
        solve_kernel,
        [(MESH, 1, CHUNK)],
        [((CHUNK // 128, MESH, 128), F32), ((PATCH_Z * SLABS, PATCH_Y * COLS), F32)],
        [plane, short, z_h, z_l, zt_h, zt_l, y_h, y_l, yt_h, yt_l],
        "solve",
        400_000_000,
        2_000_000,
        (1,),
        limit=40,
    )
    potential = lax.all_to_all(returning, BOTH, 0, 0, tiled=True)

    ghosts = back_mid + ring(back_low, "col", -1) + ring(back_high, "col", 1)
    ghosts, pos = lax.optimization_barrier((ghosts, pos))
    weights = call(
        weigh_kernel,
        [((MESH, 512), BF16), ((MESH, 512), BF16), (56, 256), (56, 256), (8, 256)],
        [((8, 256), F32)],
        [pos, kinds, count, owner, shift, basis_h, basis_l],
        "weigh",
        400_000_000,
        1_000_000,
        (2,),
        limit=40,
    )
    from_low, from_high = ring(ghosts[2], "slab", 1), ring(ghosts[0], "slab", -1)

    energy, atom_force, centre_force = call(
        interpolate_kernel,
        [(1, 128), (3, 1, ATOMS), (3, 1, CENTRES)],
        [((MESH, CHUNK), F32)],
        [potential, *weights, own, ghosts, from_low, from_high],
        "interpolate",
        600_000_000,
        1_500_000,
        limit=40,
    )
    return energy[0, 0], atom_force.reshape(1, 1, 3, ATOMS), centre_force.reshape(1, 1, 3, CENTRES)


def solution(mesh):
    return jax.shard_map(
        local,
        mesh=mesh,
        in_specs=(
            P("slab", "col", None, None),
            P("slab", "col", None),
            P("slab", "col"),
            P("slab", "col", None, None),
            P("slab", "col", None),
            P("slab", "col", None, None),
            P(),
            P(),
            P(),
            P(),
            P(),
            P(),
            P(),
            P(),
            P(),
            P(),
        ),
        out_specs=(P(), P("slab", "col", None, None), P("slab", "col", None, None)),
        check_vma=False,
    )
```
